256 devices in a mesh: grp: 8 (over z_hi, core), wide: 32 (over z_lo, y, x).
Axes of the slice: x: 4, y: 4, z: 8 (z_hi: 4, z_lo: 2; z = z_hi * 2 + z_lo), core: 2. Of those that a mesh axis runs over, the one named last changes fastest.
Arguments:
- echoes: bfloat16 [2, 128, 2048, 1024], P(None, 'wide', None, 'grp'), may hold values from -6 to 6
- patterns: bfloat16 [256, 2, 64], replicated, may hold values from -0.125 to 0.125
- block_choice: int32 [512, 16], replicated, may hold values from 0 to 255
Outputs:
- beams: bfloat16 [512, 2, 2048, 128], P('grp', None, 'wide')
The draws below stay inside these ranges and needn't reach their ends.
Inputs may be any that keep to these rules, and one draw needn't show every extreme that they name: `block_choice`: each entry names one of the 256 block patterns.
All inputs are finite; a program needn't handle non-finite values.
Results may differ from the reference program's by a relative error of at most 0.0065.
Values may be sent and summed in bfloat16 or wider, within the bound.
A program may use at most 128 MiB of HBM per device.

```python
import math
import jax
import jax.numpy as jnp
from jax import lax

PULSES = 128
CHANNELS = 1024
BLOCK = 64
PATTERNS = 256
BEAMS = 512
GATES = 2048
N_GRP = 8


def place_ends(drawn, own_key, low, top_value):
    place = [jax.random.randint(jax.random.fold_in(own_key, axis), (), 0, length) for axis, length in enumerate(drawn.shape)]
    widest = drawn.shape.index(max(drawn.shape))
    beside = place[:widest] + [(place[widest] + 1) % drawn.shape[widest]] + place[widest + 1:]
    return drawn.at[tuple(place)].set(low).at[tuple(beside)].set(top_value)


def levels(rng, shape, split, least, largest):
    gain, own = 1.0, jax.random.fold_in(rng, 6)
    for dim, parts in split:
        draws = jnp.exp(jax.random.uniform(jax.random.fold_in(own, dim), (parts,), jnp.float32, least / len(split), largest / len(split)))
        gain = gain * jnp.repeat(draws, shape[dim] // parts).reshape([-1 if axis == dim else 1 for axis in range(len(shape))])
    return gain


def bell_draw(key, dims, spread, most, cuts=(), kind=jnp.bfloat16):
    array = spread * jax.random.normal(key, dims, jnp.float32)
    if cuts:
        array = array * levels(key, dims, cuts, -0.22, 0.18)
    return jnp.clip(array, -most, most).astype(kind)


def setup_inputs(seed: int = 0) -> dict:
    streams_of = jax.random.split(jax.random.key(seed), 4)
    return {
        "echoes": bell_draw(streams_of[0], (2, PULSES, GATES, CHANNELS), 1.0, 6.0, ((1, 32), (3, 8))),
        "patterns": bell_draw(streams_of[1], (PATTERNS, 2, BLOCK), (2 * CHANNELS) ** -0.5, 0.125),
        "block_choice": place_ends(jax.random.randint(streams_of[2], (BEAMS, CHANNELS // BLOCK), 0, PATTERNS), jax.random.fold_in(streams_of[2], 1), 0, PATTERNS - 1).astype(jnp.int32),
    }


def doppler_matrix(length):
    bin_index = jnp.arange(length, dtype=jnp.int32)
    phases = bin_index[:, None] * bin_index[None, :] % length
    angles = phases.astype(jnp.float32) * (2.0 * math.pi / length)
    scale_factor = 1.0 / math.sqrt(length)
    cosine = (jnp.cos(angles) * scale_factor).astype(jnp.bfloat16)
    sine_part = (-jnp.sin(angles) * scale_factor).astype(jnp.bfloat16)
    upper_rows = jnp.stack([cosine, -sine_part], axis=1)
    lower_rows = jnp.stack([sine_part, cosine], axis=1)
    return jnp.stack([upper_rows, lower_rows], axis=0)

def steering_ref(patterns, block_choice):
    pattern_count = patterns.shape[0]
    one_hot = (block_choice[:, :, None] == jnp.arange(pattern_count, dtype=jnp.int32)[None, None, :]).astype(jnp.float32)
    picked = jnp.einsum('bjq,qot->bojt', one_hot, patterns.astype(jnp.float32)).astype(jnp.bfloat16)
    flattened = picked.reshape(picked.shape[0], 2, -1)
    real_part = flattened[:, 0]
    imag_part = flattened[:, 1]
    upper_rows = jnp.stack([real_part, -imag_part], axis=1)
    lower_rows = jnp.stack([imag_part, real_part], axis=1)
    return jnp.stack([upper_rows, lower_rows], axis=1)

def reference(echoes, patterns, block_choice):
    dft_table = doppler_matrix(PULSES).astype(jnp.float32)
    weights = steering_ref(patterns, block_choice).astype(jnp.float32)
    chan_width = CHANNELS // N_GRP
    total = jnp.zeros((BEAMS, 2, GATES, PULSES), jnp.float32)
    for group_index in range(N_GRP):
        first_chan = group_index * chan_width
        samples = echoes[:, :, :, first_chan:first_chan + chan_width].astype(jnp.float32)
        doppler = jnp.einsum('okip,iprc->ocrk', dft_table, samples).astype(jnp.bfloat16)
        doppler = lax.optimization_barrier(doppler).astype(jnp.float32)
        group_weights = weights[:, :, :, first_chan:first_chan + chan_width]
        partial_beams = jnp.einsum('boic,icrk->bork', group_weights, doppler).astype(jnp.bfloat16)
        total = total + lax.optimization_barrier(partial_beams).astype(jnp.float32)
    return total.astype(jnp.bfloat16)
```

```python
import functools
import math

import jax
import jax.numpy as jnp
import ml_dtypes
import numpy as np
from jax import lax
from jax.experimental import pallas as pl
from jax.experimental.pallas import tpu as pltpu
from jax.sharding import PartitionSpec as P

MESH = pl.DeviceIdType.MESH
CHUNKS = 2
PAIRS = 8
STRIDE = 5


def doppler_operator(length, wide):
    index = np.arange(length, dtype=np.int32)
    phases = index[:, None] * index[None, :] % length
    angles = phases.astype(np.float32) * np.float32(2.0 * math.pi / length)
    scale = np.float32(1.0 / math.sqrt(length))
    cosine = np.cos(angles) * scale
    sine = -np.sin(angles) * scale
    table = np.array([[cosine, -sine], [sine, cosine]], np.float32)
    table = table.transpose(0, 2, 1, 3).reshape(2, length, 2, wide, length // wide)
    full = np.zeros((2, 2, length, wide, 2, length // wide, 2), np.float32)
    for gate in range(2):
        full[:, gate, :, :, :, :, gate] = table.transpose(0, 1, 3, 2, 4)
    size = 4 * length
    return full.reshape(size, size).astype(ml_dtypes.bfloat16)


def pair_order():
    order = np.zeros((256, 256), np.float32)
    for block in range(2):
        for pair in range(8):
            for row in range(8):
                for gate in range(2):
                    order[block * 128 + pair * 16 + row * 2 + gate, block * 128 + row * 16 + pair * 2 + gate] = 1
    return order.astype(ml_dtypes.bfloat16)


def kernel(
    echoes, patterns, choice, operator, order, out,
    raw, turned, held, oper, perm, pats, picks, weights, dop, mine, give, got, done,
    in_sem, send_sem, recv_sem, swap_send, swap_recv, home_send, home_recv,
):
    grp, wide = lax.axis_index("grp"), lax.axis_index("wide")
    high, core = grp // 2, grp % 2
    per = PAIRS // CHUNKS

    def at(to_wide, to_high, to_core):
        return {"grp": to_high * 2 + to_core, "wide": to_wide}

    loads = [
        pltpu.make_async_copy(a, b, in_sem.at[n])
        for n, (a, b) in enumerate(
            [(echoes, raw), (order, perm), (choice, picks), (patterns, pats), (operator, oper)]
        )
    ]
    for load in loads:
        load.start()

    barrier = pltpu.get_barrier_semaphore()

    def greet(step, carry):
        pl.semaphore_signal(
            barrier,
            inc=1,
            device_id=at((wide + step // 4) % 32, (high + step % 4) % 4, core),
            device_id_type=MESH,
        )
        return carry

    lax.fori_loop(1, 128, greet, 0)
    pl.semaphore_signal(barrier, inc=1, device_id=at(wide, high, 1 - core), device_id_type=MESH)

    loads[0].wait()
    loads[1].wait()

    def turn(block, carry):
        rows = [raw[:, pl.ds(pl.multiple_of(block * 64 + n * 16, 16), 16), :].reshape(128, 128) for n in range(4)]
        both = jnp.concatenate(
            [jnp.concatenate(rows[:2], axis=0), jnp.concatenate(rows[2:], axis=0)], axis=1
        )
        moved = jnp.dot(perm[...], both, preferred_element_type=jnp.float32).astype(jnp.bfloat16)
        for n in range(4):
            part = moved[(n % 2) * 128 : (n % 2) * 128 + 128, (n // 2) * 128 : (n // 2) * 128 + 128]
            turned[block, n] = part.reshape(PAIRS, 16, 128)
        return carry

    lax.fori_loop(0, 32, turn, 0)
    pl.semaphore_wait(barrier, 128)

    def send(chunk):
        span = pl.ds(chunk * per, per)

        def one(step, carry):
            to_wide = (wide + (step // 4) * STRIDE) % 32
            to_high = (high + step % 4) % 4
            pltpu.make_async_remote_copy(
                src_ref=turned.at[to_wide, to_high, span],
                dst_ref=held.at[high, span, wide],
                send_sem=send_sem.at[chunk],
                recv_sem=recv_sem.at[chunk],
                device_id=at(to_wide, to_high, core),
                device_id_type=MESH,
            ).start()
            return carry

        lax.fori_loop(1, 128, one, 0)
        pltpu.make_async_copy(
            turned.at[wide, high, span], held.at[high, span, wide], recv_sem.at[chunk]
        ).start()

    for chunk in range(CHUNKS):
        send(chunk)

    for load in loads[2:]:
        load.wait()
    lane = lax.broadcasted_iota(jnp.int32, (512, 128), 1)
    number = lax.broadcasted_iota(jnp.int32, (512, 256), 1)
    for h in range(4):
        found = []
        for j in range(2):
            column = h * 4 + j
            pick = jnp.where(core == 0, picks[:, column : column + 1], picks[:, column + 2 : column + 3])
            hot = (pick == number).astype(jnp.float32).astype(jnp.bfloat16)
            found.append(jnp.dot(hot, pats[...], preferred_element_type=jnp.float32))
        real = jnp.where(lane < 64, found[0], pltpu.roll(found[1], 64, 1)).astype(jnp.bfloat16)
        imag = jnp.where(lane < 64, pltpu.roll(found[0], 64, 1), found[1]).astype(jnp.bfloat16)
        left, right = slice(h * 128, h * 128 + 128), slice(512 + h * 128, 512 + h * 128 + 128)
        for beams in range(8):
            rows = slice(beams * 64, beams * 64 + 64)
            upper = slice((beams // 2) * 128, (beams // 2) * 128 + 64)
            lower = slice((beams // 2) * 128 + 64, (beams // 2) * 128 + 128)
            weights[beams % 2, upper, left] = real[rows]
            weights[beams % 2, upper, right] = -imag[rows]
            weights[beams % 2, lower, left] = imag[rows]
            weights[beams % 2, lower, right] = real[rows]

    across = (((1,), (1,)), ((), ()))

    def beams_of(owner, pair):
        total = lax.dot_general(
            weights[owner, :, :512], dop[pair, :256], across, preferred_element_type=jnp.float32
        )
        return total + lax.dot_general(
            weights[owner, :, 512:], dop[pair, 256:], across, preferred_element_type=jnp.float32
        )

    def swap(pair):
        return pltpu.make_async_remote_copy(
            src_ref=give.at[pair],
            dst_ref=got.at[pair],
            send_sem=swap_send.at[pair],
            recv_sem=swap_recv.at[pair],
            device_id=at(wide, high, 1 - core),
            device_id_type=MESH,
        )

    def first(pair, carry):
        samples = jnp.concatenate([held[h, pair].reshape(512, 128) for h in range(4)], axis=1)
        dop[pair] = jnp.dot(oper[...], samples, preferred_element_type=jnp.float32).astype(jnp.bfloat16)
        give[pair] = beams_of(1 - core, pair).astype(jnp.bfloat16)
        swap(pair).start()
        return carry

    def second(pair, carry):
        mine[...] = beams_of(core, pair)
        swap(pair).wait()
        done[pair] = (mine[...] + got[pair].astype(jnp.float32)).astype(jnp.bfloat16).reshape(4, 128, 256)
        for step in (2, 1, 3):
            to_high = (high + step) % 4
            pltpu.make_async_remote_copy(
                src_ref=done.at[pair, to_high],
                dst_ref=out.at[high, pair],
                send_sem=home_send,
                recv_sem=home_recv,
                device_id=at(wide, to_high, core),
                device_id_type=MESH,
            ).start()
        pltpu.make_async_copy(done.at[pair, high], out.at[high, pair], home_recv).start()
        return carry

    for chunk in range(CHUNKS):
        arrived = held.at[:, pl.ds(chunk * per, per)]
        pltpu.make_async_copy(arrived, arrived, recv_sem.at[chunk]).wait()
        lax.fori_loop(chunk * per, chunk * per + per, first, 0)
        lax.fori_loop(chunk * per, chunk * per + per, second, 0)

    for chunk in range(CHUNKS):
        for part in (pl.ds(0, 31), pl.ds(31, 1)):
            sent = turned.at[part, :, pl.ds(chunk * per, per)]
            if part.start:
                sent = turned.at[31, pl.ds(0, 3), pl.ds(chunk * per, per)]
            pltpu.make_async_copy(sent, sent, send_sem.at[chunk]).wait()
    sent = done.at[:, pl.ds(0, 3)]
    pltpu.make_async_copy(sent, sent, home_send).wait()
    pltpu.make_async_copy(out, out, home_recv).wait()


def shards(echoes, patterns, block_choice):
    bf16 = jnp.bfloat16
    anywhere = pl.BlockSpec(memory_space=pl.ANY)
    beams = pl.pallas_call(
        kernel,
        out_shape=jax.ShapeDtypeStruct((4, PAIRS, 128, 256), bf16),
        in_specs=[anywhere] * 5,
        out_specs=anywhere,
        scratch_shapes=[
            pltpu.VMEM((8, 2048, 128), bf16),
            pltpu.VMEM((32, 4, PAIRS, 16, 128), bf16),
            pltpu.VMEM((4, PAIRS, 32, 16, 128), bf16),
            pltpu.VMEM((512, 512), bf16),
            pltpu.VMEM((256, 256), bf16),
            pltpu.VMEM((256, 128), bf16),
            pltpu.VMEM((512, 16), jnp.int32),
            pltpu.VMEM((2, 512, 1024), bf16),
            pltpu.VMEM((PAIRS, 512, 512), bf16),
            pltpu.VMEM((512, 256), jnp.float32),
            pltpu.VMEM((PAIRS, 512, 256), bf16),
            pltpu.VMEM((PAIRS, 512, 256), bf16),
            pltpu.VMEM((PAIRS, 4, 128, 256), bf16),
            pltpu.SemaphoreType.DMA((5,)),
            pltpu.SemaphoreType.DMA((CHUNKS,)),
            pltpu.SemaphoreType.DMA((CHUNKS,)),
            pltpu.SemaphoreType.DMA((PAIRS,)),
            pltpu.SemaphoreType.DMA((PAIRS,)),
            pltpu.SemaphoreType.DMA,
            pltpu.SemaphoreType.DMA,
        ],
        compiler_params=pltpu.CompilerParams(
            collective_id=0, has_side_effects=True, vmem_limit_bytes=48 << 20
        ),
    )(
        echoes.reshape(8, 2048, 128),
        patterns.reshape(256, 128),
        block_choice,
        jnp.asarray(doppler_operator(128, 32)),
        jnp.asarray(pair_order()),
    )
    return beams.reshape(4, PAIRS, 2, 64, 2, 128).transpose(3, 2, 0, 1, 4, 5).reshape(64, 2, 64, 128)


def solution(mesh):
    placed = (P(None, "wide", None, "grp"), P(), P())
    return jax.shard_map(
        shards, mesh=mesh, in_specs=placed, out_specs=P("grp", None, "wide", None), check_vma=False
    )
```

```python
import functools
import math

import jax
import jax.numpy as jnp
import ml_dtypes
import numpy as np
from jax import lax
from jax.experimental import pallas as pl
from jax.experimental.pallas import tpu as pltpu
from jax.sharding import PartitionSpec as P

MESH = pl.DeviceIdType.MESH
CHUNKS = 4
PAIRS = 8
PER = PAIRS // CHUNKS


def doppler_operator(length, wide):
    index = np.arange(length, dtype=np.int32)
    phases = index[:, None] * index[None, :] % length
    angles = phases.astype(np.float32) * np.float32(2.0 * math.pi / length)
    scale = np.float32(1.0 / math.sqrt(length))
    cosine = np.cos(angles) * scale
    sine = -np.sin(angles) * scale
    table = np.array([[cosine, -sine], [sine, cosine]], np.float32)
    table = table.transpose(0, 2, 1, 3).reshape(2, length, 2, wide, length // wide)
    full = np.zeros((2, 2, length, wide, 2, 2, length // wide), np.float32)
    for gate in range(2):
        full[:, gate, :, :, gate] = table.transpose(0, 1, 3, 2, 4)
    size = 4 * length
    return full.reshape(size, size).astype(ml_dtypes.bfloat16)


def kernel(
    echoes, patterns, choice, operator, out,
    raw, single, turned, mid, held, oper, pats, picks, weights, dop, mine, give, got, done, homed, spread, final,
    load_sem, in_sem, z_send, z_recv, xy_send, xy_recv, swap_send, swap_recv, home_send, home_recv, out_sem,
):
    grp, wide = lax.axis_index("grp"), lax.axis_index("wide")
    high, core = grp // 2, grp % 2
    low, place = wide // 16, wide % 16
    row, column = place // 4, place % 4

    def at(to_high, to_low, to_place, to_core):
        return {"grp": to_high * 2 + to_core, "wide": to_low * 16 + to_place}

    def pulled(half):
        span = pl.ds(pl.multiple_of(half * 1024, 1024), 1024)
        return pltpu.make_async_copy(echoes.at[:, span], raw.at[:, span], load_sem.at[half])

    first_half = 1 - low
    pulled(first_half).start()
    pulled(low).start()
    loads = [
        pltpu.make_async_copy(a, b, in_sem.at[n])
        for n, (a, b) in enumerate([(choice, picks), (patterns, pats), (operator, oper)])
    ]
    for load in loads:
        load.start()

    barrier = pltpu.get_barrier_semaphore()

    def greet(device):
        pl.semaphore_signal(barrier, inc=1, device_id=device, device_id_type=MESH)

    def along_z(step):
        to = (high * 2 + low + step) % 8
        return to // 2, to % 2

    def around(step):
        return ((row + step // 4) % 4) * 4 + (column + step % 4) % 4

    for step in range(1, 8):
        to_high, to_low = along_z(step)
        greet(at(to_high, to_low, place, core))
    for step in range(1, 16):
        greet(at(high, low, around(step), core))
    greet(at(high, low, place, 1 - core))

    def turn(block, carry):
        slot = block % 2
        start = pl.multiple_of(block * 64, 64)
        single[slot] = raw[:, pl.ds(start, 64), :].astype(jnp.float32)
        for h in range(4):
            for pair in range(PAIRS):
                gate = h * 16 + pair * 2
                both = jnp.concatenate([single[slot, :, gate], single[slot, :, gate + 1]], axis=0)
                turned[block, h, pair] = both.astype(jnp.bfloat16)
        return carry

    def send_z(chunk, step):
        to_high, to_low = along_z(step)
        span = pl.ds(chunk * PER, PER)
        pltpu.make_async_remote_copy(
            src_ref=turned.at[pl.ds(to_low * 16, 16), to_high, span],
            dst_ref=mid.at[:, high, span, low],
            send_sem=z_send.at[chunk],
            recv_sem=z_recv.at[chunk],
            device_id=at(to_high, to_low, place, core),
            device_id_type=MESH,
        ).start()

    def keep_z(chunk):
        span = pl.ds(chunk * PER, PER)
        pltpu.make_async_copy(
            turned.at[pl.ds(low * 16, 16), high, span], mid.at[:, high, span, low], z_recv.at[chunk]
        ).start()

    pulled(first_half).wait()
    lax.fori_loop(first_half * 16, first_half * 16 + 16, turn, 0)
    pl.semaphore_wait(barrier, 23)
    for step in (3, 5, 1, 7):
        send_z(0, step)
    pulled(low).wait()
    lax.fori_loop(low * 16, low * 16 + 16, turn, 0)
    for step in (4, 2, 6):
        send_z(0, step)
    keep_z(0)
    for chunk in range(1, CHUNKS):
        for step in (4, 3, 5, 2, 6, 1, 7):
            send_z(chunk, step)
        keep_z(chunk)

    def send_xy(chunk):
        span = pl.ds(chunk * PER, PER)
        arrived = mid.at[:, :, span]
        pltpu.make_async_copy(arrived, arrived, z_recv.at[chunk]).wait()

        def one(step, carry):
            to = around(step)
            pltpu.make_async_remote_copy(
                src_ref=mid.at[to, :, span],
                dst_ref=held.at[:, span, :, place],
                send_sem=xy_send.at[chunk],
                recv_sem=xy_recv.at[chunk],
                device_id=at(high, low, to, core),
                device_id_type=MESH,
            ).start()
            return carry

        lax.fori_loop(1, 16, one, 0)
        pltpu.make_async_copy(
            mid.at[place, :, span], held.at[:, span, :, place], xy_recv.at[chunk]
        ).start()

    for load in loads:
        load.wait()
    lane = lax.broadcasted_iota(jnp.int32, (512, 128), 1)
    number = lax.broadcasted_iota(jnp.int32, (256, 512), 0)
    for h in range(4):
        found = []
        for j in range(2):
            n = h * 4 + j
            pick = jnp.where(core == 0, picks[n : n + 1, :], picks[n + 2 : n + 3, :])
            hot = (pick == number).astype(jnp.float32).astype(jnp.bfloat16)
            found.append(jnp.dot(pats[...], hot, preferred_element_type=jnp.float32).T)
        real = jnp.where(lane < 64, found[0], pltpu.roll(found[1], 64, 1)).astype(jnp.bfloat16)
        imag = jnp.where(lane < 64, pltpu.roll(found[0], 64, 1), found[1]).astype(jnp.bfloat16)
        left, right = slice(h * 128, h * 128 + 128), slice(512 + h * 128, 512 + h * 128 + 128)
        for beams in range(8):
            rows = slice(beams * 64, beams * 64 + 64)
            upper = slice((beams // 2) * 128, (beams // 2) * 128 + 64)
            lower = slice((beams // 2) * 128 + 64, (beams // 2) * 128 + 128)
            weights[beams % 2, upper, left] = real[rows]
            weights[beams % 2, upper, right] = -imag[rows]
            weights[beams % 2, lower, left] = imag[rows]
            weights[beams % 2, lower, right] = real[rows]

    across = (((1,), (1,)), ((), ()))

    def beams_of(owner, pair):
        total = lax.dot_general(
            weights[owner, :, :512], dop[pair, :256], across, preferred_element_type=jnp.float32
        )
        return total + lax.dot_general(
            weights[owner, :, 512:], dop[pair, 256:], across, preferred_element_type=jnp.float32
        )

    def swap(pair):
        return pltpu.make_async_remote_copy(
            src_ref=give.at[pair],
            dst_ref=got.at[pair],
            send_sem=swap_send.at[pair],
            recv_sem=swap_recv.at[pair],
            device_id=at(high, low, place, 1 - core),
            device_id_type=MESH,
        )

    def first(pair, carry):
        samples = jnp.concatenate([held[h, pair].reshape(512, 128) for h in range(4)], axis=1)
        dop[pair] = jnp.dot(oper[...], samples, preferred_element_type=jnp.float32).astype(jnp.bfloat16)
        give[pair] = beams_of(1 - core, pair).astype(jnp.bfloat16)
        swap(pair).start()
        return carry

    def work(chunk):
        span = pl.ds(chunk * PER, PER)
        arrived = held.at[:, span]
        pltpu.make_async_copy(arrived, arrived, xy_recv.at[chunk]).wait()
        start = chunk * PER

        def second(pair, carry):
            mine[...] = beams_of(core, pair)
            swap(pair).wait()
            done[pair] = (mine[...] + got[pair].astype(jnp.float32)).astype(jnp.bfloat16).reshape(4, 128, 256)
            for step in (2, 1, 3):
                to_high = (high + step) % 4
                pltpu.make_async_remote_copy(
                    src_ref=done.at[pair, to_high],
                    dst_ref=homed.at[high, pair],
                    send_sem=home_send,
                    recv_sem=home_recv.at[high, chunk],
                    device_id=at(to_high, low, place, core),
                    device_id_type=MESH,
                ).start()
            pltpu.make_async_copy(
                done.at[pair, high], homed.at[high, pair], home_recv.at[high, chunk]
            ).start()
            return carry

        lax.fori_loop(start, start + PER, first, 0)
        lax.fori_loop(start, start + PER, second, 0)

    send_xy(0)
    for chunk in range(1, CHUNKS):
        send_xy(chunk)
        work(chunk - 1)
    work(CHUNKS - 1)

    for chunk in range(CHUNKS):
        for step in range(4):
            source = (high + step) % 4
            span = pl.ds(chunk * PER, PER)
            landed = homed.at[source, span]
            pltpu.make_async_copy(landed, landed, home_recv.at[source, chunk]).wait()
            for pair in range(chunk * PER, chunk * PER + PER):
                for gate in range(2):
                    piece = homed[source, pair, :, gate * 128 : gate * 128 + 128]
                    spread[source, :, pair * 2 + gate, :] = piece.astype(jnp.float32)
            if chunk == CHUNKS - 1:
                final[source] = spread[source].astype(jnp.bfloat16)
                for part in range(2):
                    pltpu.make_async_copy(
                        final.at[source, pl.ds(part * 64, 64)],
                        out.at[:, part, pl.ds(pl.multiple_of(source * 16, 16), 16)],
                        out_sem,
                    ).start()

    for chunk in range(CHUNKS):
        span = pl.ds(chunk * PER, PER)
        for part in (pl.ds(0, 16), pl.ds(16, 8), pl.ds(24, 4)):
            sent = turned.at[part, :, span]
            pltpu.make_async_copy(sent, sent, z_send.at[chunk]).wait()
        sent = mid.at[pl.ds(0, 15), :, span]
        pltpu.make_async_copy(sent, sent, xy_send.at[chunk]).wait()
    sent = done.at[:, pl.ds(0, 3)]
    pltpu.make_async_copy(sent, sent, home_send).wait()
    pltpu.make_async_copy(out, out, out_sem).wait()


def shards(echoes, patterns, block_choice):
    bf16, f32 = jnp.bfloat16, jnp.float32
    anywhere = pl.BlockSpec(memory_space=pl.ANY)
    return pl.pallas_call(
        kernel,
        out_shape=jax.ShapeDtypeStruct((64, 2, 64, 128), bf16),
        in_specs=[anywhere] + [pl.BlockSpec(memory_space=pltpu.HBM)] * 3,
        out_specs=anywhere,
        scratch_shapes=[
            pltpu.VMEM((8, 2048, 128), bf16),
            pltpu.VMEM((2, 8, 64, 128), f32),
            pltpu.VMEM((32, 4, PAIRS, 16, 128), bf16),
            pltpu.VMEM((16, 4, PAIRS, 2, 16, 128), bf16),
            pltpu.VMEM((4, PAIRS, 2, 16, 16, 128), bf16),
            pltpu.VMEM((512, 512), bf16),
            pltpu.VMEM((128, 256), bf16),
            pltpu.VMEM((16, 512), jnp.int32),
            pltpu.VMEM((2, 512, 1024), bf16),
            pltpu.VMEM((PAIRS, 512, 512), bf16),
            pltpu.VMEM((512, 256), f32),
            pltpu.VMEM((PAIRS, 512, 256), bf16),
            pltpu.VMEM((PAIRS, 512, 256), bf16),
            pltpu.VMEM((PAIRS, 4, 128, 256), bf16),
            pltpu.VMEM((4, PAIRS, 128, 256), bf16),
            pltpu.VMEM((4, 128, 16, 128), f32),
            pltpu.VMEM((4, 128, 16, 128), bf16),
            pltpu.SemaphoreType.DMA((2,)),
            pltpu.SemaphoreType.DMA((3,)),
            pltpu.SemaphoreType.DMA((CHUNKS,)),
            pltpu.SemaphoreType.DMA((CHUNKS,)),
            pltpu.SemaphoreType.DMA((CHUNKS,)),
            pltpu.SemaphoreType.DMA((CHUNKS,)),
            pltpu.SemaphoreType.DMA((PAIRS,)),
            pltpu.SemaphoreType.DMA((PAIRS,)),
            pltpu.SemaphoreType.DMA,
            pltpu.SemaphoreType.DMA((4, CHUNKS)),
            pltpu.SemaphoreType.DMA,
        ],
        compiler_params=pltpu.CompilerParams(
            collective_id=0, has_side_effects=True, vmem_limit_bytes=48 << 20
        ),
    )(
        echoes.reshape(8, 2048, 128),
        patterns.transpose(1, 2, 0).reshape(128, 256),
        block_choice.T,
        jnp.asarray(doppler_operator(128, 32)),
    )


def solution(mesh):
    placed = (P(None, "wide", None, "grp"), P(), P())
    return jax.shard_map(
        shards, mesh=mesh, in_specs=placed, out_specs=P("grp", None, "wide", None), check_vma=False
    )
```

```python
import math

import jax
import jax.numpy as jnp
import ml_dtypes
import numpy as np
from jax import lax
from jax.experimental import pallas as pl
from jax.experimental.pallas import tpu as pltpu
from jax.sharding import PartitionSpec as P

MESH = pl.DeviceIdType.MESH
CHUNKS = 4


def doppler_operator(length, wide):
    index = np.arange(length, dtype=np.int32)
    phases = index[:, None] * index[None, :] % length
    angles = phases.astype(np.float32) * np.float32(2.0 * math.pi / length)
    scale = np.float32(1.0 / math.sqrt(length))
    cosine = np.cos(angles) * scale
    sine = -np.sin(angles) * scale
    table = np.array([[cosine, -sine], [sine, cosine]], np.float32)
    table = table.transpose(0, 2, 1, 3).reshape(2, length, 2, wide, length // wide)
    full = np.zeros((2, 2, length, wide, 2, 2, length // wide), np.float32)
    for gate in range(2):
        full[:, gate, :, :, gate] = table.transpose(0, 1, 3, 2, 4)
    halves = full.reshape(4 * length, 2, 2 * length).transpose(1, 0, 2)
    return halves.astype(ml_dtypes.bfloat16)


def kernel(
    echoes, patterns, choice, operator, out,
    raw, single, turned, mid, held, oper, pats, picks, weights, dop, mine, give, got, keep, pass_on, passed, done,
    homed, spread, final,
    load_sem, in_sem, z_send, z_recv, xy_send, xy_recv, swap_send, swap_recv, pass_send, pass_recv, home_send, home_recv,
    out_sem,
):
    grp, wide = lax.axis_index("grp"), lax.axis_index("wide")
    high, core = grp // 2, grp % 2
    low, place = wide // 16, wide % 16
    row, column = place // 4, place % 4
    plane = high * 2 + low

    def at(to_plane, to_place, to_core):
        return {"grp": (to_plane // 2) * 2 + to_core, "wide": (to_plane % 2) * 16 + to_place}

    def away(step):
        return (plane + step + 8) % 8

    def around(step):
        return ((row + step // 4) % 4) * 4 + (column + step % 4) % 4

    def await_all(ref, sem):
        pltpu.make_async_copy(ref, ref, sem).wait()

    loads = [
        pltpu.make_async_copy(echoes.at[:, pl.ds(n * 1024, 1024)], raw.at[:, pl.ds(n * 1024, 1024)], load_sem.at[n])
        for n in range(2)
    ]
    small = [
        pltpu.make_async_copy(a, b, in_sem.at[n])
        for n, (a, b) in enumerate([(choice, picks), (patterns, pats), (operator, oper)])
    ]
    for load in loads + small:
        load.start()

    barrier = pltpu.get_barrier_semaphore()

    def greet(device):
        pl.semaphore_signal(barrier, inc=1, device_id=device, device_id_type=MESH)

    for step in (-3, -2, -1, 1, 2, 3):
        greet(at(away(step), place, core))
    for step in range(1, 16):
        greet(at(plane, around(step), core))
    greet(at(plane, place, 1 - core))

    def turn(block, carry):
        slot = block % 2
        single[slot] = raw[:, pl.ds(pl.multiple_of(block * 64, 64), 64), :].astype(jnp.float32)
        for eighth in range(8):
            for chunk in range(CHUNKS):
                gate = eighth * 8 + chunk * 2
                both = jnp.concatenate([single[slot, :, gate], single[slot, :, gate + 1]], axis=0)
                turned[block % 16, block // 16, eighth, chunk] = both.astype(jnp.bfloat16)
        return carry

    for n in range(2):
        loads[n].wait()
        lax.fori_loop(n * 16, n * 16 + 16, turn, 0)
    pl.semaphore_wait(barrier, 22)

    for chunk in range(CHUNKS):
        for step in (3, -3, 2, -2, 1, -1):
            side = 0 if step > 0 else 1
            eighth = away(step) if step > 0 else away(step - 1)
            pltpu.make_async_remote_copy(
                src_ref=turned.at[:, :, eighth, chunk],
                dst_ref=mid.at[:, side, abs(step), :, chunk],
                send_sem=z_send.at[chunk],
                recv_sem=z_recv.at[chunk],
                device_id=at(away(step), place, core),
                device_id_type=MESH,
            ).start()
        for side in range(2):
            pltpu.make_async_copy(
                turned.at[:, :, away(-side), chunk], mid.at[:, side, 0, :, chunk], z_recv.at[chunk]
            ).start()

    def send_xy(chunk):
        await_all(mid.at[:, :, :, :, chunk], z_recv.at[chunk])

        def one(step, carry):
            to = around(step)
            pltpu.make_async_remote_copy(
                src_ref=mid.at[to, :, :, :, chunk],
                dst_ref=held.at[:, :, :, chunk, place],
                send_sem=xy_send.at[chunk],
                recv_sem=xy_recv.at[chunk],
                device_id=at(plane, to, core),
                device_id_type=MESH,
            ).start()
            return carry

        lax.fori_loop(1, 16, one, 0)
        pltpu.make_async_copy(
            mid.at[place, :, :, :, chunk], held.at[:, :, :, chunk, place], xy_recv.at[chunk]
        ).start()

    for load in small:
        load.wait()
    lane = lax.broadcasted_iota(jnp.int32, (512, 128), 1)
    number = lax.broadcasted_iota(jnp.int32, (256, 512), 0)
    for h in range(4):
        found = []
        for j in range(2):
            n = h * 4 + j
            pick = jnp.where(core == 0, picks[n : n + 1, :], picks[n + 2 : n + 3, :])
            hot = (pick == number).astype(jnp.float32).astype(jnp.bfloat16)
            found.append(jnp.dot(pats[...], hot, preferred_element_type=jnp.float32).T)
        real = jnp.where(lane < 64, found[0], pltpu.roll(found[1], 64, 1)).astype(jnp.bfloat16)
        imag = jnp.where(lane < 64, pltpu.roll(found[0], 64, 1), found[1]).astype(jnp.bfloat16)
        for beams in range(8):
            rows = slice(beams * 64, beams * 64 + 64)
            upper = slice((beams // 2) * 128, (beams // 2) * 128 + 64)
            lower = slice((beams // 2) * 128 + 64, (beams // 2) * 128 + 128)
            weights[beams % 2, h, upper, :128] = real[rows]
            weights[beams % 2, h, upper, 128:] = -imag[rows]
            weights[beams % 2, h, lower, :128] = imag[rows]
            weights[beams % 2, h, lower, 128:] = real[rows]

    def beams_of(owner, n):
        side = n // 2
        used = [weights[owner, away((2 * side - 1) * unit) // 2] for unit in range(4)]
        return lax.dot_general(
            jnp.concatenate(used, axis=1), dop[n], (((1,), (1,)), ((), ())), preferred_element_type=jnp.float32
        )

    def swap(chunk, n):
        return pltpu.make_async_remote_copy(
            src_ref=give.at[chunk, n],
            dst_ref=got.at[chunk, n],
            send_sem=swap_send.at[chunk, n],
            recv_sem=swap_recv.at[chunk, n],
            device_id=at(plane, place, 1 - core),
            device_id_type=MESH,
        )

    def hand(chunk, n):
        side, other = n // 2, n % 2
        to = (1 - side) * 2 + 1 - other
        return pltpu.make_async_remote_copy(
            src_ref=pass_on.at[chunk, n],
            dst_ref=passed.at[chunk, to],
            send_sem=pass_send.at[chunk, n],
            recv_sem=pass_recv.at[chunk, to],
            device_id=at(away(1 - 2 * side), place, core),
            device_id_type=MESH,
        )

    def partials(chunk):
        await_all(held.at[:, :, :, chunk], xy_recv.at[chunk])

        def first(n, carry):
            side, half = n // 2, (low + n) % 2
            samples = [held[side, unit, half, chunk].reshape(256, 128) for unit in range(4)]
            bins = []
            for odd in range(2):
                both = jnp.concatenate([samples[odd], samples[odd + 2]], axis=1)
                bins.append(
                    jnp.dot(oper[(low + odd) % 2], both, preferred_element_type=jnp.float32).astype(jnp.bfloat16)
                )
            parts = []
            for unit in range(4):
                of = bins[unit % 2][:, (unit // 2) * 128 : (unit // 2) * 128 + 128]
                parts += [of[:256], of[256:]]
            dop[n] = jnp.concatenate(parts, axis=1)
            give[chunk, n] = beams_of(1 - core, n).astype(jnp.bfloat16)
            swap(chunk, n).start()
            return carry

        def second(n, carry):
            mine[...] = beams_of(core, n).reshape(4, 128, 256)
            swap(chunk, n).wait()
            side, other = n // 2, n % 2
            ahead = 2 * side - 1
            for e in range(2):
                h = away(ahead * (other + 2 * e)) // 2
                keep[chunk, n, e] = mine[h] + got[chunk, n, pl.ds(pl.multiple_of(h * 128, 128), 128)].astype(jnp.float32)
                h = away(-ahead * (2 - other + 2 * e)) // 2
                both = mine[h] + got[chunk, n, pl.ds(pl.multiple_of(h * 128, 128), 128)].astype(jnp.float32)
                pass_on[chunk, n, e] = both.astype(jnp.bfloat16)
            hand(chunk, n).start()
            return carry

        lax.fori_loop(0, 4, first, 0)
        lax.fori_loop(0, 4, second, 0)

    def send_home(chunk):
        for n in range(4):
            side, other = n // 2, n % 2
            ahead = 2 * side - 1
            await_all(passed.at[chunk, n], pass_recv.at[chunk, n])
            for e in range(2):
                both = keep[chunk, n, e] + passed[chunk, n, e].astype(jnp.float32)
                done[chunk, n, e] = both.astype(jnp.bfloat16)
                far = other + 2 * e
                slot = 7 - far if side else far
                if far == 0:
                    pltpu.make_async_copy(
                        done.at[chunk, n, e], homed.at[slot, chunk], home_recv.at[slot, chunk]
                    ).start()
                else:
                    pltpu.make_async_remote_copy(
                        src_ref=done.at[chunk, n, e],
                        dst_ref=homed.at[slot, chunk],
                        send_sem=home_send,
                        recv_sem=home_recv.at[slot, chunk],
                        device_id=at(away(ahead * far), place, core),
                        device_id_type=MESH,
                    ).start()

    send_xy(0)

    def forward(chunk, carry):
        @pl.when(chunk < CHUNKS - 1)
        def _():
            send_xy(chunk + 1)

        @pl.when(chunk == CHUNKS - 1)
        def _():
            for earlier in range(CHUNKS - 1):
                send_home(earlier)

        partials(chunk)
        return carry

    lax.fori_loop(0, CHUNKS, forward, 0)
    send_home(CHUNKS - 1)

    for chunk in range(CHUNKS):

        def place_gates(eighth, carry):
            slot = (eighth - plane + 8) % 8
            await_all(homed.at[slot, chunk], home_recv.at[slot, chunk])
            for gate in range(2):
                piece = homed[slot, chunk, :, gate * 128 : gate * 128 + 128]
                spread[eighth, :, chunk * 2 + gate, :] = piece.astype(jnp.float32)
            return carry

        if chunk < CHUNKS - 1:
            lax.fori_loop(0, 8, place_gates, 0)
        else:
            for quarter in range(4):
                lax.fori_loop(quarter * 2, quarter * 2 + 2, place_gates, 0)
                rows = jnp.concatenate([spread[quarter * 2], spread[quarter * 2 + 1]], axis=1)
                final[quarter] = rows.astype(jnp.bfloat16)
                for part in range(2):
                    pltpu.make_async_copy(
                        final.at[quarter, pl.ds(part * 64, 64)],
                        out.at[:, part, pl.ds(quarter * 16, 16)],
                        out_sem,
                    ).start()

    for chunk in range(CHUNKS):
        await_all(turned.at[:, :, pl.ds(0, 6), chunk], z_send.at[chunk])
        await_all(mid.at[pl.ds(0, 15), :, :, :, chunk], xy_send.at[chunk])
        for n in range(4):
            await_all(pass_on.at[chunk, n], pass_send.at[chunk, n])
    await_all(homed.at[pl.ds(0, 6)], home_send)
    await_all(out, out_sem)


def shards(echoes, patterns, block_choice):
    bf16, f32 = jnp.bfloat16, jnp.float32
    anywhere = pl.BlockSpec(memory_space=pl.ANY)
    small = [
        patterns.transpose(1, 2, 0).reshape(128, 256),
        block_choice.T,
        jnp.asarray(doppler_operator(128, 32)),
    ]
    return pl.pallas_call(
        kernel,
        out_shape=jax.ShapeDtypeStruct((64, 2, 64, 128), bf16),
        in_specs=[anywhere] * 4,
        out_specs=anywhere,
        scratch_shapes=[
            pltpu.VMEM((8, 2048, 128), bf16),
            pltpu.VMEM((2, 8, 64, 128), f32),
            pltpu.VMEM((16, 2, 8, CHUNKS, 16, 128), bf16),
            pltpu.VMEM((16, 2, 4, 2, CHUNKS, 16, 128), bf16),
            pltpu.VMEM((2, 4, 2, CHUNKS, 16, 16, 128), bf16),
            pltpu.VMEM((2, 512, 256), bf16),
            pltpu.VMEM((128, 256), bf16),
            pltpu.VMEM((16, 512), jnp.int32),
            pltpu.VMEM((2, 4, 512, 256), bf16),
            pltpu.VMEM((4, 256, 1024), bf16),
            pltpu.VMEM((4, 128, 256), f32),
            pltpu.VMEM((CHUNKS, 4, 512, 256), bf16),
            pltpu.VMEM((CHUNKS, 4, 512, 256), bf16),
            pltpu.VMEM((CHUNKS, 4, 2, 128, 256), f32),
            pltpu.VMEM((CHUNKS, 4, 2, 128, 256), bf16),
            pltpu.VMEM((CHUNKS, 4, 2, 128, 256), bf16),
            pltpu.VMEM((CHUNKS, 4, 2, 128, 256), bf16),
            pltpu.VMEM((8, CHUNKS, 128, 256), bf16),
            pltpu.VMEM((8, 128, 8, 128), f32),
            pltpu.VMEM((4, 128, 16, 128), bf16),
            pltpu.SemaphoreType.DMA((2,)),
            pltpu.SemaphoreType.DMA((3,)),
            pltpu.SemaphoreType.DMA((CHUNKS,)),
            pltpu.SemaphoreType.DMA((CHUNKS,)),
            pltpu.SemaphoreType.DMA((CHUNKS,)),
            pltpu.SemaphoreType.DMA((CHUNKS,)),
            pltpu.SemaphoreType.DMA((CHUNKS, 4)),
            pltpu.SemaphoreType.DMA((CHUNKS, 4)),
            pltpu.SemaphoreType.DMA((CHUNKS, 4)),
            pltpu.SemaphoreType.DMA((CHUNKS, 4)),
            pltpu.SemaphoreType.DMA,
            pltpu.SemaphoreType.DMA((8, CHUNKS)),
            pltpu.SemaphoreType.DMA,
        ],
        compiler_params=pltpu.CompilerParams(
            collective_id=0, has_side_effects=True, vmem_limit_bytes=49 << 20
        ),
    )(
        echoes.reshape(8, 2048, 128),
        *[pltpu.with_memory_space_constraint(array, pltpu.HBM) for array in small],
    )


def solution(mesh):
    placed = (P(None, "wide", None, "grp"), P(), P())
    return jax.shard_map(
        shards, mesh=mesh, in_specs=placed, out_specs=P("grp", None, "wide", None), check_vma=False
    )
```

```python
import math

import jax
import jax.numpy as jnp
import ml_dtypes
import numpy as np
from jax import lax
from jax.experimental import pallas as pl
from jax.experimental.pallas import tpu as pltpu
from jax.sharding import PartitionSpec as P

MESH = pl.DeviceIdType.MESH
CHUNKS = 4


def doppler_operator(length, wide):
    index = np.arange(length, dtype=np.int32)
    phases = index[:, None] * index[None, :] % length
    angles = phases.astype(np.float32) * np.float32(2.0 * math.pi / length)
    scale = np.float32(1.0 / math.sqrt(length))
    cosine = np.cos(angles) * scale
    sine = -np.sin(angles) * scale
    table = np.array([[cosine, -sine], [sine, cosine]], np.float32)
    table = table.transpose(0, 2, 1, 3).reshape(2, length, 2, wide, length // wide)
    full = np.zeros((2, 2, length, wide, 2, 2, length // wide), np.float32)
    for gate in range(2):
        full[:, gate, :, :, gate] = table.transpose(0, 1, 3, 2, 4)
    halves = full.reshape(4 * length, 2, 2 * length).transpose(1, 0, 2)
    return halves.astype(ml_dtypes.bfloat16)


def kernel(
    echoes, patterns, choice, operator, out,
    raw, single, turned, mid, held, oper, pats, picks, weights, dop, mine, give, got, keep, pass_on, passed, done,
    homed, spread, final,
    load_sem, in_sem, z_send, z_recv, xy_send, xy_recv, swap_send, swap_recv, pass_send, pass_recv, home_send, home_recv,
    out_sem,
):
    grp, wide = lax.axis_index("grp"), lax.axis_index("wide")
    high, core = grp // 2, grp % 2
    low, place = wide // 16, wide % 16
    row, column = place // 4, place % 4
    plane = high * 2 + low

    def at(to_plane, to_place, to_core):
        return {"grp": (to_plane // 2) * 2 + to_core, "wide": (to_plane % 2) * 16 + to_place}

    def away(step):
        return (plane + step + 8) % 8

    def around(step):
        return ((row + step // 4) % 4) * 4 + (column + step % 4) % 4

    def await_all(ref, sem):
        pltpu.make_async_copy(ref, ref, sem).wait()

    quarters = [(high + step) % 4 for step in (1, 3, 2, 0)]
    loads = [
        pltpu.make_async_copy(echoes.at[:, :, quarter], raw.at[n], load_sem.at[n])
        for n, quarter in enumerate(quarters)
    ]
    small = [
        pltpu.make_async_copy(a, b, in_sem.at[n])
        for n, (a, b) in enumerate([(choice, picks), (patterns, pats), (operator, oper)])
    ]
    loads[0].start()

    barrier = pltpu.get_barrier_semaphore()

    def greet(device):
        pl.semaphore_signal(barrier, inc=1, device_id=device, device_id_type=MESH)

    for step in (-3, -2, -1, 1, 2, 3):
        greet(at(away(step), place, core))
    for step in range(1, 16):
        greet(at(plane, around(step), core))
    greet(at(plane, place, 1 - core))

    for load in loads[1:] + small:
        load.start()

    def turn(n, block):
        slot = block % 4
        single[slot] = raw[n, :, block].astype(jnp.float32)
        for eighth in range(2):
            for chunk in range(CHUNKS):
                gate = eighth * 8 + chunk * 2
                both = jnp.concatenate([single[slot, :, gate], single[slot, :, gate + 1]], axis=0)
                turned[block % 16, block // 16, quarters[n] * 2 + eighth, chunk] = both.astype(jnp.bfloat16)

    def send_z(eighth, chunk):
        ahead = (eighth - plane + 8) % 8
        side = ahead // 4
        unit = ahead + side * (7 - 2 * ahead)

        @pl.when(unit > 0)
        def _():
            pltpu.make_async_remote_copy(
                src_ref=turned.at[:, :, eighth, chunk],
                dst_ref=mid.at[:, side, unit, :, chunk],
                send_sem=z_send.at[chunk],
                recv_sem=z_recv.at[chunk],
                device_id=at(away(ahead - 7 * side), place, core),
                device_id_type=MESH,
            ).start()

    for n in range(4):
        loads[n].wait()

        def turn_some(some, carry):
            for block in range(4):
                turn(n, some * 4 + block)
            return carry

        lax.fori_loop(0, 8, turn_some, 0)
        if n == 0:
            pl.semaphore_wait(barrier, 22)
        for eighth in range(2):
            send_z(quarters[n] * 2 + eighth, 0)
    for chunk in range(CHUNKS):
        if chunk:
            for step in (3, 4, 2, 5, 1, 6):
                send_z(away(step), chunk)
        for side in range(2):
            pltpu.make_async_copy(
                turned.at[:, :, away(-side), chunk], mid.at[:, side, 0, :, chunk], z_recv.at[chunk]
            ).start()

    def send_xy(chunk):
        await_all(mid.at[:, :, :, :, chunk], z_recv.at[chunk])

        def one(step, carry):
            to = around(step)
            pltpu.make_async_remote_copy(
                src_ref=mid.at[to, :, :, :, chunk],
                dst_ref=held.at[:, :, :, chunk, place],
                send_sem=xy_send.at[chunk],
                recv_sem=xy_recv.at[chunk],
                device_id=at(plane, to, core),
                device_id_type=MESH,
            ).start()
            return carry

        lax.fori_loop(1, 16, one, 0)
        pltpu.make_async_copy(
            mid.at[place, :, :, :, chunk], held.at[:, :, :, chunk, place], xy_recv.at[chunk]
        ).start()

    for load in small:
        load.wait()
    lane = lax.broadcasted_iota(jnp.int32, (512, 128), 1)
    number = lax.broadcasted_iota(jnp.int32, (256, 512), 0)
    for h in range(4):
        found = []
        for j in range(2):
            n = h * 4 + j
            pick = jnp.where(core == 0, picks[n : n + 1, :], picks[n + 2 : n + 3, :])
            hot = (pick == number).astype(jnp.float32).astype(jnp.bfloat16)
            found.append(jnp.dot(pats[...], hot, preferred_element_type=jnp.float32).T)
        real = jnp.where(lane < 64, found[0], pltpu.roll(found[1], 64, 1)).astype(jnp.bfloat16)
        imag = jnp.where(lane < 64, pltpu.roll(found[0], 64, 1), found[1]).astype(jnp.bfloat16)
        for beams in range(8):
            rows = slice(beams * 64, beams * 64 + 64)
            upper = slice((beams // 2) * 128, (beams // 2) * 128 + 64)
            lower = slice((beams // 2) * 128 + 64, (beams // 2) * 128 + 128)
            weights[beams % 2, h, upper, :128] = real[rows]
            weights[beams % 2, h, upper, 128:] = -imag[rows]
            weights[beams % 2, h, lower, :128] = imag[rows]
            weights[beams % 2, h, lower, 128:] = real[rows]

    def beams_of(owner, n):
        side = n // 2
        used = [weights[owner, away((2 * side - 1) * unit) // 2] for unit in range(4)]
        return lax.dot_general(
            jnp.concatenate(used, axis=1), dop[n], (((1,), (1,)), ((), ())), preferred_element_type=jnp.float32
        )

    def swap(chunk, n):
        return pltpu.make_async_remote_copy(
            src_ref=give.at[chunk, n],
            dst_ref=got.at[chunk, n],
            send_sem=swap_send.at[chunk, n],
            recv_sem=swap_recv.at[chunk, n],
            device_id=at(plane, place, 1 - core),
            device_id_type=MESH,
        )

    def hand(chunk, n):
        side, other = n // 2, n % 2
        to = (1 - side) * 2 + 1 - other
        return pltpu.make_async_remote_copy(
            src_ref=pass_on.at[chunk, n],
            dst_ref=passed.at[chunk, to],
            send_sem=pass_send.at[chunk, n],
            recv_sem=pass_recv.at[chunk, to],
            device_id=at(away(1 - 2 * side), place, core),
            device_id_type=MESH,
        )

    def partials(chunk):
        await_all(held.at[:, :, :, chunk], xy_recv.at[chunk])

        def first(n, carry):
            side, half = n // 2, (low + n) % 2
            samples = [held[side, unit, half, chunk].reshape(256, 128) for unit in range(4)]
            bins = []
            for odd in range(2):
                both = jnp.concatenate([samples[odd], samples[odd + 2]], axis=1)
                bins.append(
                    jnp.dot(oper[(low + odd) % 2], both, preferred_element_type=jnp.float32).astype(jnp.bfloat16)
                )
            parts = []
            for unit in range(4):
                of = bins[unit % 2][:, (unit // 2) * 128 : (unit // 2) * 128 + 128]
                parts += [of[:256], of[256:]]
            dop[n] = jnp.concatenate(parts, axis=1)
            give[chunk, n] = beams_of(1 - core, n).astype(jnp.bfloat16)
            swap(chunk, n).start()
            return carry

        def second(n, carry):
            mine[...] = beams_of(core, n).reshape(4, 128, 256)
            swap(chunk, n).wait()
            side, other = n // 2, n % 2
            ahead = 2 * side - 1
            for e in range(2):
                h = away(ahead * (other + 2 * e)) // 2
                keep[chunk, n, e] = mine[h] + got[chunk, n, pl.ds(pl.multiple_of(h * 128, 128), 128)].astype(jnp.float32)
                h = away(-ahead * (2 - other + 2 * e)) // 2
                both = mine[h] + got[chunk, n, pl.ds(pl.multiple_of(h * 128, 128), 128)].astype(jnp.float32)
                pass_on[chunk, n, e] = both.astype(jnp.bfloat16)

            @pl.when(chunk > 0)
            def _():
                hand(chunk, n).start()

            return carry

        lax.fori_loop(0, 4, first, 0)
        lax.fori_loop(0, 4, second, 0)

    def send_home(chunk):
        for n in range(4):
            side, other = n // 2, n % 2
            ahead = 2 * side - 1
            await_all(passed.at[chunk, n], pass_recv.at[chunk, n])
            for e in range(2):
                both = keep[chunk, n, e] + passed[chunk, n, e].astype(jnp.float32)
                done[chunk, n, e] = both.astype(jnp.bfloat16)
                far = other + 2 * e
                slot = 7 - far if side else far
                if far == 0:
                    pltpu.make_async_copy(
                        done.at[chunk, n, e], homed.at[slot, chunk], home_recv.at[slot, chunk]
                    ).start()
                else:
                    pltpu.make_async_remote_copy(
                        src_ref=done.at[chunk, n, e],
                        dst_ref=homed.at[slot, chunk],
                        send_sem=home_send,
                        recv_sem=home_recv.at[slot, chunk],
                        device_id=at(away(ahead * far), place, core),
                        device_id_type=MESH,
                    ).start()

    send_xy(0)

    def forward(chunk, carry):
        @pl.when(chunk < CHUNKS - 1)
        def _():
            send_xy(chunk + 1)

        @pl.when(chunk == CHUNKS - 2)
        def _():
            for n in range(4):
                hand(0, n).start()

        @pl.when(chunk == CHUNKS - 1)
        def _():
            for earlier in range(CHUNKS - 2):
                send_home(earlier)

        partials(chunk)
        return carry

    lax.fori_loop(0, CHUNKS, forward, 0)
    send_home(CHUNKS - 2)
    send_home(CHUNKS - 1)

    for chunk in range(CHUNKS):

        def place_gates(eighth, carry):
            slot = (eighth - plane + 8) % 8
            await_all(homed.at[slot, chunk], home_recv.at[slot, chunk])
            for gate in range(2):
                piece = homed[slot, chunk, :, gate * 128 : gate * 128 + 128]
                spread[eighth, :, chunk * 2 + gate, :] = piece.astype(jnp.float32)
            return carry

        if chunk < CHUNKS - 1:
            lax.fori_loop(0, 8, place_gates, 0)
        else:
            for quarter in range(4):
                lax.fori_loop(quarter * 2, quarter * 2 + 2, place_gates, 0)
                rows = jnp.concatenate([spread[quarter * 2], spread[quarter * 2 + 1]], axis=1)
                final[quarter] = rows.astype(jnp.bfloat16)
                for part in range(2):
                    pltpu.make_async_copy(
                        final.at[quarter, pl.ds(part * 64, 64)],
                        out.at[:, part, pl.ds(quarter * 16, 16)],
                        out_sem,
                    ).start()

    for chunk in range(CHUNKS):
        await_all(turned.at[:, :, pl.ds(0, 6), chunk], z_send.at[chunk])
        await_all(mid.at[pl.ds(0, 15), :, :, :, chunk], xy_send.at[chunk])
        for n in range(4):
            await_all(pass_on.at[chunk, n], pass_send.at[chunk, n])
    await_all(homed.at[pl.ds(0, 6)], home_send)
    await_all(out, out_sem)


def shards(echoes, patterns, block_choice):
    bf16, f32 = jnp.bfloat16, jnp.float32
    anywhere = pl.BlockSpec(memory_space=pl.ANY)
    small = [
        patterns.transpose(1, 2, 0).reshape(128, 256),
        block_choice.T,
        jnp.asarray(doppler_operator(128, 32)),
    ]
    return pl.pallas_call(
        kernel,
        out_shape=jax.ShapeDtypeStruct((64, 2, 64, 128), bf16),
        in_specs=[anywhere] * 4,
        out_specs=anywhere,
        scratch_shapes=[
            pltpu.VMEM((4, 8, 32, 16, 128), bf16),
            pltpu.VMEM((4, 8, 16, 128), f32),
            pltpu.VMEM((16, 2, 8, CHUNKS, 16, 128), bf16),
            pltpu.VMEM((16, 2, 4, 2, CHUNKS, 16, 128), bf16),
            pltpu.VMEM((2, 4, 2, CHUNKS, 16, 16, 128), bf16),
            pltpu.VMEM((2, 512, 256), bf16),
            pltpu.VMEM((128, 256), bf16),
            pltpu.VMEM((16, 512), jnp.int32),
            pltpu.VMEM((2, 4, 512, 256), bf16),
            pltpu.VMEM((4, 256, 1024), bf16),
            pltpu.VMEM((4, 128, 256), f32),
            pltpu.VMEM((CHUNKS, 4, 512, 256), bf16),
            pltpu.VMEM((CHUNKS, 4, 512, 256), bf16),
            pltpu.VMEM((CHUNKS, 4, 2, 128, 256), f32),
            pltpu.VMEM((CHUNKS, 4, 2, 128, 256), bf16),
            pltpu.VMEM((CHUNKS, 4, 2, 128, 256), bf16),
            pltpu.VMEM((CHUNKS, 4, 2, 128, 256), bf16),
            pltpu.VMEM((8, CHUNKS, 128, 256), bf16),
            pltpu.VMEM((8, 128, 8, 128), f32),
            pltpu.VMEM((4, 128, 16, 128), bf16),
            pltpu.SemaphoreType.DMA((4,)),
            pltpu.SemaphoreType.DMA((3,)),
            pltpu.SemaphoreType.DMA((CHUNKS,)),
            pltpu.SemaphoreType.DMA((CHUNKS,)),
            pltpu.SemaphoreType.DMA((CHUNKS,)),
            pltpu.SemaphoreType.DMA((CHUNKS,)),
            pltpu.SemaphoreType.DMA((CHUNKS, 4)),
            pltpu.SemaphoreType.DMA((CHUNKS, 4)),
            pltpu.SemaphoreType.DMA((CHUNKS, 4)),
            pltpu.SemaphoreType.DMA((CHUNKS, 4)),
            pltpu.SemaphoreType.DMA,
            pltpu.SemaphoreType.DMA((8, CHUNKS)),
            pltpu.SemaphoreType.DMA,
        ],
        compiler_params=pltpu.CompilerParams(
            collective_id=0, has_side_effects=True, vmem_limit_bytes=49 << 20
        ),
    )(
        echoes.reshape(8, 32, 4, 16, 128),
        *[pltpu.with_memory_space_constraint(array, pltpu.HBM) for array in small],
    )


def solution(mesh):
    placed = (P(None, "wide", None, "grp"), P(), P())
    return jax.shard_map(
        shards, mesh=mesh, in_specs=placed, out_specs=P("grp", None, "wide", None), check_vma=False
    )
```

```python
import math

import jax
import jax.numpy as jnp
import ml_dtypes
import numpy as np
from jax import lax
from jax.experimental import pallas as pl
from jax.experimental.pallas import tpu as pltpu
from jax.sharding import PartitionSpec as P

MESH = pl.DeviceIdType.MESH
CHUNKS = 4


def doppler_operator(length, wide):
    index = np.arange(length, dtype=np.int32)
    phases = index[:, None] * index[None, :] % length
    angles = phases.astype(np.float32) * np.float32(2.0 * math.pi / length)
    scale = np.float32(1.0 / math.sqrt(length))
    cosine = np.cos(angles) * scale
    sine = -np.sin(angles) * scale
    table = np.array([[cosine, -sine], [sine, cosine]], np.float32)
    table = table.transpose(0, 2, 1, 3).reshape(2, length, 2, wide, length // wide)
    full = np.zeros((2, 2, length, wide, 2, 2, length // wide), np.float32)
    for gate in range(2):
        full[:, gate, :, :, gate] = table.transpose(0, 1, 3, 2, 4)
    halves = full.reshape(4 * length, 2, 2 * length).transpose(1, 0, 2)
    return halves.astype(ml_dtypes.bfloat16)


def kernel(
    echoes, patterns, choice, operator, out,
    raw, single, turned, mid, held, oper, pats, picks, weights, dop, mine, give, got, keep, kept, to_middle, at_middle,
    back, passed, homed, spread,
    load_sem, in_sem, z_send, z_recv, xy_send, xy_recv, swap_send, swap_recv, middle_send, middle_recv, back_send,
    back_recv, home_send, home_recv, out_sem,
):
    grp, wide = lax.axis_index("grp"), lax.axis_index("wide")
    high, core = grp // 2, grp % 2
    low, place = wide // 16, wide % 16
    row, column = place // 4, place % 4
    plane = high * 2 + low

    def at(to_plane, to_place, to_core):
        return {"grp": (to_plane // 2) * 2 + to_core, "wide": (to_plane % 2) * 16 + to_place}

    def away(step):
        return (plane + step + 8) % 8

    def around(step):
        return ((row + step // 4) % 4) * 4 + (column + step % 4) % 4

    def await_all(ref, sem):
        pltpu.make_async_copy(ref, ref, sem).wait()

    quarters = [(high + step) % 4 for step in (1, 3, 2, 0)]
    loads = [
        pltpu.make_async_copy(echoes.at[:, quarter], raw.at[n], load_sem.at[n])
        for n, quarter in enumerate(quarters)
    ]
    small = [
        pltpu.make_async_copy(a, b, in_sem.at[n])
        for n, (a, b) in enumerate([(choice, picks), (patterns, pats), (operator, oper)])
    ]
    loads[0].start()

    barrier = pltpu.get_barrier_semaphore()

    def greet(device):
        pl.semaphore_signal(barrier, inc=1, device_id=device, device_id_type=MESH)

    for step in (-3, -2, -1, 1, 2, 3):
        greet(at(away(step), place, core))
    for step in range(1, 16):
        greet(at(plane, around(step), core))
    greet(at(plane, place, 1 - core))

    for load in loads[1:] + small:
        load.start()

    def turn(n, block):
        slot = block % 4
        for ip in range(8):
            single[slot, ip] = raw[n, ip * 32 + block].astype(jnp.float32)
        for eighth in range(2):
            for chunk in range(CHUNKS):
                gate = eighth * 8 + chunk * 2
                both = jnp.concatenate([single[slot, :, gate], single[slot, :, gate + 1]], axis=0)
                turned[block % 16, block // 16, quarters[n] * 2 + eighth, chunk] = both.astype(jnp.bfloat16)

    def send_z(eighth, chunk):
        ahead = (eighth - plane + 8) % 8
        side = ahead // 4
        unit = ahead + side * (7 - 2 * ahead)

        def to_worker(role):
            far = unit - role

            @pl.when(far > 0)
            def _():
                pltpu.make_async_remote_copy(
                    src_ref=turned.at[:, (low + far) % 2, eighth, chunk],
                    dst_ref=mid.at[:, side * 8 + role * 4 + far, chunk],
                    send_sem=z_send.at[chunk],
                    recv_sem=z_recv.at[chunk],
                    device_id=at(away((1 - 2 * side) * far), place, core),
                    device_id_type=MESH,
                ).start()

        to_worker(0)
        to_worker(1)

    def keep_z(chunk):
        for side in range(2):
            for slot, half, eighth in ((0, low, -side), (4, low, 1 - 3 * side), (7, 1 - low, -side)):
                pltpu.make_async_copy(
                    turned.at[:, half, away(eighth), chunk], mid.at[:, side * 8 + slot, chunk], z_recv.at[chunk]
                ).start()

    for n in range(4):
        loads[n].wait()

        def turn_some(some, carry):
            for block in range(4):
                turn(n, some * 4 + block)
            return carry

        lax.fori_loop(0, 8, turn_some, 0)
        if n == 0:
            pl.semaphore_wait(barrier, 22)
        for eighth in range(2):
            send_z(quarters[n] * 2 + eighth, 0)
    for chunk in range(CHUNKS):
        if chunk:
            for step in (3, 4, 2, 5, 1, 6):
                send_z(away(step), chunk)
        keep_z(chunk)

    def send_xy(chunk):
        await_all(mid.at[:, :, chunk], z_recv.at[chunk])

        def one(step, carry):
            to = around(step)
            pltpu.make_async_remote_copy(
                src_ref=mid.at[to, :, chunk],
                dst_ref=held.at[:, chunk, place],
                send_sem=xy_send.at[chunk],
                recv_sem=xy_recv.at[chunk],
                device_id=at(plane, to, core),
                device_id_type=MESH,
            ).start()
            return carry

        lax.fori_loop(1, 16, one, 0)
        pltpu.make_async_copy(mid.at[place, :, chunk], held.at[:, chunk, place], xy_recv.at[chunk]).start()

    for load in small:
        load.wait()
    lane = lax.broadcasted_iota(jnp.int32, (512, 128), 1)
    number = lax.broadcasted_iota(jnp.int32, (256, 512), 0)
    for h in range(4):
        found = []
        for j in range(2):
            n = h * 4 + j
            pick = jnp.where(core == 0, picks[n : n + 1, :], picks[n + 2 : n + 3, :])
            hot = (pick == number).astype(jnp.float32).astype(jnp.bfloat16)
            found.append(jnp.dot(pats[...], hot, preferred_element_type=jnp.float32).T)
        real = jnp.where(lane < 64, found[0], pltpu.roll(found[1], 64, 1)).astype(jnp.bfloat16)
        imag = jnp.where(lane < 64, pltpu.roll(found[0], 64, 1), found[1]).astype(jnp.bfloat16)
        for beams in range(8):
            rows = slice(beams * 64, beams * 64 + 64)
            upper = slice((beams // 2) * 128, (beams // 2) * 128 + 64)
            lower = slice((beams // 2) * 128 + 64, (beams // 2) * 128 + 128)
            weights[beams % 2, h, upper, :128] = real[rows]
            weights[beams % 2, h, upper, 128:] = -imag[rows]
            weights[beams % 2, h, lower, :128] = imag[rows]
            weights[beams % 2, h, lower, 128:] = real[rows]

    units = (4, 3, 1)

    def beams_of(owner, role, side):
        used = [weights[owner, away((2 * side - 1) * unit) // 2] for unit in range(units[role])]
        return lax.dot_general(
            jnp.concatenate(used, axis=1),
            dop[role, side, :, : units[role] * 256],
            (((1,), (1,)), ((), ())),
            preferred_element_type=jnp.float32,
        )

    def swap(chunk, role, side):
        return pltpu.make_async_remote_copy(
            src_ref=give.at[role, side],
            dst_ref=got.at[chunk % 2, role, side],
            send_sem=swap_send.at[chunk, role, side],
            recv_sem=swap_recv.at[chunk, role, side],
            device_id=at(plane, place, 1 - core),
            device_id_type=MESH,
        )

    def hand(chunk, role, side):
        to = (1 - side, side)[role]
        return pltpu.make_async_remote_copy(
            src_ref=to_middle.at[chunk, role, side],
            dst_ref=at_middle.at[chunk, role, to],
            send_sem=middle_send.at[chunk, role, side],
            recv_sem=middle_recv.at[chunk, role, to],
            device_id=at(away(1 - 2 * side), place, core),
            device_id_type=MESH,
        )

    def hand_back(chunk, role, side):
        to = (1 - side, side)[role]
        return pltpu.make_async_remote_copy(
            src_ref=back.at[chunk, role, side],
            dst_ref=passed.at[chunk, role, to],
            send_sem=back_send.at[chunk, role, side],
            recv_sem=back_recv.at[chunk, role, to],
            device_id=at(away((1 - 2 * side, 2 * side - 1)[role]), place, core),
            device_id_type=MESH,
        )

    def partials(chunk):
        await_all(held.at[:, chunk], xy_recv.at[chunk])

        def first(role, side):
            samples = [held[side * 8 + role * 4 - role // 2 + unit, chunk].reshape(256, 128) for unit in range(units[role])]
            bins = []
            for odd in range(min(units[role], 2)):
                both = jnp.concatenate(samples[odd::2], axis=1)
                bins.append(
                    jnp.dot(oper[(low + odd) % 2], both, preferred_element_type=jnp.float32).astype(jnp.bfloat16)
                )
            parts = []
            for unit in range(units[role]):
                of = bins[unit % 2][:, (unit // 2) * 128 : (unit // 2) * 128 + 128]
                parts += [of[:256], of[256:]]
            dop[role, side, :, : units[role] * 256] = jnp.concatenate(parts, axis=1)
            give[role, side] = beams_of(1 - core, role, side).astype(jnp.bfloat16)
            swap(chunk, role, side).start()

        def second(role, side):
            mine[...] = beams_of(core, role, side).reshape(4, 128, 256)
            swap(chunk, role, side).wait()
            ahead = 2 * side - 1

            def combined(step):
                h = away(step) // 2
                rows = pl.ds(pl.multiple_of(h * 128, 128), 128)
                return mine[h] + got[chunk % 2, role, side, rows].astype(jnp.float32)

            for e in range(2):
                if role == 2:
                    kept[chunk % 2, 0, side, e] = combined(-ahead * (1 + 2 * e))
                    kept[chunk % 2, 1, side, e] = combined(ahead * (1 + 2 * e))
                else:
                    keep[chunk, role, side, e] = combined(ahead * 2 * e)
                    to_middle[chunk, role, side, e] = combined(-ahead * (2 + 2 * e)).astype(jnp.bfloat16)
            if role < 2:
                hand(chunk, role, side).start()

        def both_sides(step, role):
            def one(side, carry):
                step(role, side)
                return carry

            lax.fori_loop(0, 2, one, 0)

        for step in (first, second):
            for role in range(3):
                both_sides(step, role)

    def add_middle(chunk):
        for role in range(2):
            for side in range(2):
                await_all(at_middle.at[chunk, 1 - role, side], middle_recv.at[chunk, 1 - role, side])
                for e in range(2):
                    both = kept[chunk % 2, role, side, e] + at_middle[chunk, 1 - role, side, e].astype(jnp.float32)
                    back[chunk, role, side, e] = both.astype(jnp.bfloat16)
                hand_back(chunk, role, side).start()

    def send_home(chunk):
        for role in range(2):
            for side in range(2):
                await_all(passed.at[chunk, role, side], back_recv.at[chunk, role, side])
                await_all(to_middle.at[chunk, role, side], middle_send.at[chunk, role, side])
                for e in (1, 0):
                    both = keep[chunk, role, side, e] + passed[chunk, role, side, e].astype(jnp.float32)
                    to_middle[chunk, role, side, e] = both.astype(jnp.bfloat16)
                    slot = 7 - role - 2 * e if side else role + 2 * e
                    if e == 0:
                        pltpu.make_async_copy(
                            to_middle.at[chunk, role, side, e], homed.at[slot, chunk], home_recv.at[slot, chunk]
                        ).start()
                    else:
                        pltpu.make_async_remote_copy(
                            src_ref=to_middle.at[chunk, role, side, e],
                            dst_ref=homed.at[slot, chunk],
                            send_sem=home_send,
                            recv_sem=home_recv.at[slot, chunk],
                            device_id=at(away((2 * side - 1) * 2), place, core),
                            device_id_type=MESH,
                        ).start()

    send_xy(0)

    def forward(chunk, carry):
        @pl.when(chunk < CHUNKS - 1)
        def _():
            send_xy(chunk + 1)

        @pl.when(chunk == CHUNKS - 2)
        def _():
            add_middle(0)

        @pl.when(chunk == CHUNKS - 1)
        def _():
            add_middle(1)
            send_home(0)

        partials(chunk)
        return carry

    lax.fori_loop(0, CHUNKS, forward, 0)
    add_middle(CHUNKS - 2)
    send_home(CHUNKS - 3)
    add_middle(CHUNKS - 1)
    send_home(CHUNKS - 2)
    send_home(CHUNKS - 1)

    for chunk in range(CHUNKS):

        def place_gates(eighth, carry):
            slot = (eighth - plane + 8) % 8
            await_all(homed.at[slot, chunk], home_recv.at[slot, chunk])
            for gate in range(2):
                piece = homed[slot, chunk, :, gate * 128 : gate * 128 + 128]
                spread[eighth, :, chunk * 2 + gate, :] = piece.astype(jnp.float32)
            return carry

        if chunk < CHUNKS - 1:
            lax.fori_loop(0, 8, place_gates, 0)
        else:
            for quarter in range(4):
                lax.fori_loop(quarter * 2, quarter * 2 + 2, place_gates, 0)
                rows = jnp.concatenate([spread[quarter * 2], spread[quarter * 2 + 1]], axis=1)
                raw[quarter, :128] = rows.astype(jnp.bfloat16)
                for part in range(2):
                    pltpu.make_async_copy(
                        raw.at[quarter, pl.ds(part * 64, 64)],
                        out.at[:, part, pl.ds(quarter * 16, 16)],
                        out_sem,
                    ).start()

    for chunk in range(CHUNKS):
        await_all(mid.at[:, pl.ds(0, 10), chunk], z_send.at[chunk])
        await_all(mid.at[pl.ds(0, 15), :, chunk], xy_send.at[chunk])
        for role in range(2):
            for side in range(2):
                await_all(back.at[chunk, role, side], back_send.at[chunk, role, side])
    await_all(homed.at[pl.ds(0, 4)], home_send)
    await_all(out, out_sem)


def shards(echoes, patterns, block_choice):
    bf16, f32 = jnp.bfloat16, jnp.float32
    anywhere = pl.BlockSpec(memory_space=pl.ANY)
    small = [
        patterns.transpose(1, 2, 0).reshape(128, 256),
        block_choice.T,
        jnp.asarray(doppler_operator(128, 32)),
    ]
    return pl.pallas_call(
        kernel,
        out_shape=jax.ShapeDtypeStruct((64, 2, 64, 128), bf16),
        in_specs=[anywhere] * 4,
        out_specs=anywhere,
        scratch_shapes=[
            pltpu.VMEM((4, 256, 16, 128), bf16),
            pltpu.VMEM((4, 8, 16, 128), f32),
            pltpu.VMEM((16, 2, 8, CHUNKS, 16, 128), bf16),
            pltpu.VMEM((16, 16, CHUNKS, 16, 128), bf16),
            pltpu.VMEM((16, CHUNKS, 16, 16, 128), bf16),
            pltpu.VMEM((2, 512, 256), bf16),
            pltpu.VMEM((128, 256), bf16),
            pltpu.VMEM((16, 512), jnp.int32),
            pltpu.VMEM((2, 4, 512, 256), bf16),
            pltpu.VMEM((3, 2, 256, 1024), bf16),
            pltpu.VMEM((4, 128, 256), f32),
            pltpu.VMEM((3, 2, 512, 256), bf16),
            pltpu.VMEM((2, 3, 2, 512, 256), bf16),
            pltpu.VMEM((CHUNKS, 2, 2, 2, 128, 256), f32),
            pltpu.VMEM((2, 2, 2, 2, 128, 256), f32),
            pltpu.VMEM((CHUNKS, 2, 2, 2, 128, 256), bf16),
            pltpu.VMEM((CHUNKS, 2, 2, 2, 128, 256), bf16),
            pltpu.VMEM((CHUNKS, 2, 2, 2, 128, 256), bf16),
            pltpu.VMEM((CHUNKS, 2, 2, 2, 128, 256), bf16),
            pltpu.VMEM((8, CHUNKS, 128, 256), bf16),
            pltpu.VMEM((8, 128, 8, 128), f32),
            pltpu.SemaphoreType.DMA((4,)),
            pltpu.SemaphoreType.DMA((3,)),
            pltpu.SemaphoreType.DMA((CHUNKS,)),
            pltpu.SemaphoreType.DMA((CHUNKS,)),
            pltpu.SemaphoreType.DMA((CHUNKS,)),
            pltpu.SemaphoreType.DMA((CHUNKS,)),
            pltpu.SemaphoreType.DMA((CHUNKS, 3, 2)),
            pltpu.SemaphoreType.DMA((CHUNKS, 3, 2)),
            pltpu.SemaphoreType.DMA((CHUNKS, 2, 2)),
            pltpu.SemaphoreType.DMA((CHUNKS, 2, 2)),
            pltpu.SemaphoreType.DMA((CHUNKS, 2, 2)),
            pltpu.SemaphoreType.DMA((CHUNKS, 2, 2)),
            pltpu.SemaphoreType.DMA,
            pltpu.SemaphoreType.DMA((8, CHUNKS)),
            pltpu.SemaphoreType.DMA,
        ],
        compiler_params=pltpu.CompilerParams(
            collective_id=0, has_side_effects=True, vmem_limit_bytes=50 << 20
        ),
    )(
        echoes.reshape(256, 4, 16, 128),
        *[pltpu.with_memory_space_constraint(array, pltpu.HBM) for array in small],
    )


def solution(mesh):
    placed = (P(None, "wide", None, "grp"), P(), P())
    return jax.shard_map(
        shards, mesh=mesh, in_specs=placed, out_specs=P("grp", None, "wide", None), check_vma=False
    )
```

```python
import math

import jax
import jax.numpy as jnp
import ml_dtypes
import numpy as np
from jax import lax
from jax.experimental import pallas as pl
from jax.experimental.pallas import tpu as pltpu
from jax.sharding import PartitionSpec as P

MESH = pl.DeviceIdType.MESH
CHUNKS = 4


def doppler_operator(length, wide):
    index = np.arange(length, dtype=np.int32)
    phases = index[:, None] * index[None, :] % length
    angles = phases.astype(np.float32) * np.float32(2.0 * math.pi / length)
    scale = np.float32(1.0 / math.sqrt(length))
    cosine = np.cos(angles) * scale
    sine = -np.sin(angles) * scale
    table = np.array([[cosine, -sine], [sine, cosine]], np.float32)
    table = table.transpose(0, 2, 1, 3).reshape(2, length, 2, wide, length // wide)
    full = np.zeros((2, 2, length, wide, 2, 2, length // wide), np.float32)
    for gate in range(2):
        full[:, gate, :, :, gate] = table.transpose(0, 1, 3, 2, 4)
    return full.reshape(4 * length, 4 * length).T.reshape(2, 2 * length, 4 * length).astype(ml_dtypes.bfloat16)


def kernel(
    echoes, patterns, choice, operator, out,
    raw, single, turned, mid, held, oper, pats, picks, weights, mine, give, got, keep, pass_on, passed, keep_odd,
    pass_odd, passed_odd, to_mid, sums, near, far, home, home_odd, home_mid, spread,
    load_sem, in_sem, z_send, z_recv, xy_send, xy_recv, swap_send, swap_recv, pass_send, pass_recv, odd_send, odd_recv,
    mid_send, mid_recv, sums_send, sums_recv, near_send, near_recv, far_send, far_recv, out_sem,
):
    grp, wide = lax.axis_index("grp"), lax.axis_index("wide")
    high, core = grp // 2, grp % 2
    low, place = wide // 16, wide % 16
    row, column = place // 4, place % 4
    plane = high * 2 + low

    def at(to_plane, to_place, to_core):
        return {"grp": (to_plane // 2) * 2 + to_core, "wide": (to_plane % 2) * 16 + to_place}

    def away(step):
        return (plane + step + 8) % 8

    def around(step):
        return ((row + step // 4) % 4) * 4 + (column + step % 4) % 4

    def await_all(ref, sem):
        pltpu.make_async_copy(ref, ref, sem).wait()

    quarters = [(high + step) % 4 for step in (1, 2, 3, 0)]
    loads = [
        pltpu.make_async_copy(echoes.at[:, quarter], raw.at[n], load_sem.at[n])
        for n, quarter in enumerate(quarters)
    ]
    small = [
        pltpu.make_async_copy(a, b, in_sem.at[n])
        for n, (a, b) in enumerate([(choice, picks), (patterns, pats), (operator, oper)])
    ]
    loads[0].start()

    barrier = pltpu.get_barrier_semaphore()

    def greet(device):
        pl.semaphore_signal(barrier, inc=1, device_id=device, device_id_type=MESH)

    for step in (-3, -2, -1, 1, 2, 3):
        greet(at(away(step), place, core))
    for step in range(1, 16):
        greet(at(plane, around(step), core))
    greet(at(plane, place, 1 - core))

    for load in loads[1:] + small:
        load.start()

    def turn(n, block):
        slot = block % 4
        for ip in range(8):
            single[slot, ip] = raw[n, ip * 32 + block].astype(jnp.float32)
        for pair in range(8):
            both = jnp.concatenate([single[slot, :, pair * 2], single[slot, :, pair * 2 + 1]], axis=0)
            turned[block % 16, block // 16, quarters[n], pair] = both.astype(jnp.bfloat16)

    def of(chunk):
        return pl.ds(chunk * 2, 2)

    def send_z(chunk, side):
        pltpu.make_async_remote_copy(
            src_ref=turned.at[:, :, quarters[side], of(chunk)],
            dst_ref=mid.at[:, side, 1, :, of(chunk)],
            send_sem=z_send.at[chunk],
            recv_sem=z_recv.at[chunk],
            device_id=at(away(2 - 4 * side), place, core),
            device_id_type=MESH,
        ).start()

    for n in range(4):
        loads[n].wait()

        def turn_some(some, carry):
            for block in range(4):
                turn(n, some * 4 + block)
            return carry

        lax.fori_loop(0, 8, turn_some, 0)
        if n == 0:
            pl.semaphore_wait(barrier, 22)
        for chunk in range(CHUNKS):
            if n < 2:
                send_z(chunk, n)
            else:
                side = 3 - n
                pltpu.make_async_copy(
                    turned.at[:, :, quarters[n], of(chunk)], mid.at[:, side, 0, :, of(chunk)], z_recv.at[chunk]
                ).start()

    def send_xy(chunk):
        await_all(mid.at[:, :, :, :, of(chunk)], z_recv.at[chunk])

        def one(step, carry):
            to = around(step)
            pltpu.make_async_remote_copy(
                src_ref=mid.at[to, :, :, :, of(chunk)],
                dst_ref=held.at[:, :, :, of(chunk), place],
                send_sem=xy_send.at[chunk],
                recv_sem=xy_recv.at[chunk],
                device_id=at(plane, to, core),
                device_id_type=MESH,
            ).start()
            return carry

        lax.fori_loop(1, 16, one, 0)
        pltpu.make_async_copy(
            mid.at[place, :, :, :, of(chunk)], held.at[:, :, :, of(chunk), place], xy_recv.at[chunk]
        ).start()

    for load in small:
        load.wait()
    lane = lax.broadcasted_iota(jnp.int32, (512, 128), 1)
    number = lax.broadcasted_iota(jnp.int32, (256, 512), 0)
    for h in range(4):
        found = []
        for j in range(2):
            n = h * 4 + j
            pick = jnp.where(core == 0, picks[n : n + 1, :], picks[n + 2 : n + 3, :])
            hot = (pick == number).astype(jnp.float32).astype(jnp.bfloat16)
            found.append(jnp.dot(pats[...], hot, preferred_element_type=jnp.float32).T)
        real = jnp.where(lane < 64, found[0], pltpu.roll(found[1], 64, 1)).astype(jnp.bfloat16)
        imag = jnp.where(lane < 64, pltpu.roll(found[0], 64, 1), found[1]).astype(jnp.bfloat16)
        for beams in range(8):
            rows = slice(beams * 64, beams * 64 + 64)
            to = slice((beams // 2) * 64, (beams // 2) * 64 + 64)
            weights[beams % 2, h, 0, to] = real[rows]
            weights[beams % 2, h, 1, to] = imag[rows]

    real_lane = lax.broadcasted_iota(jnp.int32, (256, 256), 1) // 4 % 2 == 0

    def beams_of(owner, chunk, n):
        side, half, pair = n // 4, (low + n // 2) % 2, chunk * 2 + n % 2
        used = [weights[owner, h].reshape(512, 128) for h in (high, (high + 2 * side + 3) % 4)]
        samples = [held[side, unit, half, pair].reshape(256, 128) for unit in range(2)]
        both = lax.dot_general(
            jnp.concatenate(used, axis=1),
            jnp.concatenate(samples, axis=1),
            (((1,), (1,)), ((), ())),
            preferred_element_type=jnp.float32,
        )
        by_real, by_imag = both[:256], both[256:]
        return by_real + jnp.where(real_lane, -pltpu.roll(by_imag, 252, 1), pltpu.roll(by_imag, 4, 1))

    def remote(source, target, send, recv, step):
        return pltpu.make_async_remote_copy(
            src_ref=source,
            dst_ref=target,
            send_sem=send,
            recv_sem=recv,
            device_id=at(away(step), place, core),
            device_id_type=MESH,
        )

    def swap(chunk, n):
        return pltpu.make_async_remote_copy(
            src_ref=give.at[n],
            dst_ref=got.at[chunk % 2, n],
            send_sem=swap_send.at[chunk, n],
            recv_sem=swap_recv.at[chunk, n],
            device_id=at(plane, place, 1 - core),
            device_id_type=MESH,
        )

    def partials(chunk):
        await_all(held.at[:, :, :, of(chunk)], xy_recv.at[chunk])

        def first(n, carry):
            give[n] = beams_of(1 - core, chunk, n).astype(jnp.bfloat16)
            swap(chunk, n).start()
            return carry

        def second(side, carry):
            ahead = 2 * side - 1
            for other in range(2):
                for j in range(2):
                    n = side * 4 + other * 2 + j
                    mine[...] = beams_of(core, chunk, n).reshape(4, 64, 256)
                    swap(chunk, n).wait()

                    def combined(step):
                        h = away(step) // 2
                        rows = pl.ds(pl.multiple_of(h * 64, 64), 64)
                        return mine[h] + got[chunk % 2, n, rows].astype(jnp.float32)

                    if other == 0:
                        for e in range(2):
                            keep[chunk, side, j, e] = combined(ahead * 2 * e)
                            pass_on[chunk, side, j, e] = combined(-ahead * (2 + 2 * e)).astype(jnp.bfloat16)
                    else:
                        keep_odd[chunk, side, j] = combined(ahead)
                        pass_odd[chunk, side, j] = combined(-ahead * 3).astype(jnp.bfloat16)
                        to_mid[chunk, side, j] = combined(-ahead).astype(jnp.bfloat16)

                        @pl.when(side == j)
                        def _():
                            keep_odd[chunk, side, 2] = combined(ahead * 3)

                        @pl.when(side != j)
                        def _():
                            pass_odd[chunk, side, 2] = combined(ahead * 3).astype(jnp.bfloat16)

            remote(
                pass_on.at[chunk, side], passed.at[chunk, 1 - side],
                pass_send.at[chunk, side], pass_recv.at[chunk, 1 - side], -2 * ahead,
            ).start()
            remote(
                pass_odd.at[chunk, side], passed_odd.at[chunk, 1 - side],
                odd_send.at[chunk, side], odd_recv.at[chunk, 1 - side], -2 * ahead,
            ).start()
            remote(
                to_mid.at[chunk, side], home_mid.at[side, of(chunk)],
                mid_send.at[chunk, side], mid_recv.at[chunk, side], -ahead,
            ).start()
            return carry

        lax.fori_loop(0, 8, first, 0)
        lax.fori_loop(0, 2, second, 0)

    def combine(chunk):
        for side in range(2):
            ahead = 2 * side - 1
            await_all(passed_odd.at[chunk, side], odd_recv.at[chunk, side])
            both = keep_odd[chunk, side] + passed_odd[chunk, side].astype(jnp.float32)
            far[chunk, side] = both[2].astype(jnp.bfloat16)
            remote(
                far.at[chunk, side], home_odd.at[1, chunk * 2 + side],
                far_send.at[chunk, side], far_recv.at[chunk, side], 3 * ahead,
            ).start()
            near[chunk, side] = both[:2].astype(jnp.bfloat16)
            remote(
                near.at[chunk, side], home_odd.at[2 * side, of(chunk)],
                near_send.at[chunk, side], near_recv.at[chunk, side], ahead,
            ).start()
            await_all(passed.at[chunk, side], pass_recv.at[chunk, side])
            for j in range(2):
                both = keep[chunk, side, j] + passed[chunk, side, j].astype(jnp.float32)
                home[3 * side, chunk * 2 + j] = both[0].astype(jnp.bfloat16)
                sums[chunk, side, j] = both[1].astype(jnp.bfloat16)
            remote(
                sums.at[chunk, side], home.at[1 + side, of(chunk)],
                sums_send.at[chunk, side], sums_recv.at[chunk, side], 2 * ahead,
            ).start()

    send_xy(0)

    def forward(chunk, carry):
        @pl.when(chunk < CHUNKS - 1)
        def _():
            send_xy(chunk + 1)

        for late in range(2, CHUNKS):

            @pl.when(chunk == late)
            def _():
                combine(late - 2)

        partials(chunk)
        return carry

    lax.fori_loop(0, CHUNKS, forward, 0)
    combine(CHUNKS - 2)
    combine(CHUNKS - 1)

    for chunk in range(CHUNKS):
        for side in range(2):
            await_all(home_mid.at[side, of(chunk)], mid_recv.at[chunk, side])
            await_all(home_odd.at[2 * side, of(chunk)], near_recv.at[chunk, side])
            await_all(home_odd.at[1, chunk * 2 + side], far_recv.at[chunk, side])
        both = home_mid[0, of(chunk)].astype(jnp.float32) + home_mid[1, of(chunk)].astype(jnp.float32)
        home_odd[3, of(chunk)] = both.astype(jnp.bfloat16)
        for slot in (0, 3, 1, 2):
            if slot in (1, 2):
                await_all(home.at[slot, of(chunk)], sums_recv.at[chunk, slot - 1])
            quarter = (high + slot) % 4
            same = home[slot, of(chunk)].reshape(128, 256)
            others = home_odd[(slot + 4 - low) % 4, of(chunk)].reshape(128, 256)
            bins = jnp.dot(same, oper[low], preferred_element_type=jnp.float32)
            bins += jnp.dot(others, oper[1 - low], preferred_element_type=jnp.float32)
            for j in range(2):
                for o in range(2):
                    for gate in range(2):
                        piece = bins[j * 64 : j * 64 + 64, (o * 2 + gate) * 128 : (o * 2 + gate) * 128 + 128]
                        spread[quarter, o * 64 : o * 64 + 64, (chunk * 2 + j) * 2 + gate, :] = piece
            if chunk == CHUNKS - 1:
                raw[quarter, :128] = spread[quarter].astype(jnp.bfloat16)
                for o in range(2):
                    pltpu.make_async_copy(
                        raw.at[quarter, pl.ds(o * 64, 64)],
                        out.at[:, o, pl.ds(pl.multiple_of(quarter * 16, 16), 16)],
                        out_sem,
                    ).start()

    for chunk in range(CHUNKS):
        await_all(turned.at[:, :, pl.ds(0, 2), of(chunk)], z_send.at[chunk])
        await_all(mid.at[pl.ds(0, 15), :, :, :, of(chunk)], xy_send.at[chunk])
        for side in range(2):
            for ref, sem in (
                (pass_on, pass_send), (pass_odd, odd_send), (to_mid, mid_send), (sums, sums_send), (near, near_send),
                (far, far_send),
            ):
                await_all(ref.at[chunk, side], sem.at[chunk, side])
    await_all(out, out_sem)


def shards(echoes, patterns, block_choice):
    bf16, f32 = jnp.bfloat16, jnp.float32
    anywhere = pl.BlockSpec(memory_space=pl.ANY)
    small = [
        patterns.transpose(1, 2, 0).reshape(128, 256),
        block_choice.T,
        jnp.asarray(doppler_operator(128, 32)),
    ]
    return pl.pallas_call(
        kernel,
        out_shape=jax.ShapeDtypeStruct((64, 2, 64, 128), bf16),
        in_specs=[anywhere] * 4,
        out_specs=anywhere,
        scratch_shapes=[
            pltpu.VMEM((4, 256, 16, 128), bf16),
            pltpu.VMEM((4, 8, 16, 128), f32),
            pltpu.VMEM((16, 2, 4, 8, 16, 128), bf16),
            pltpu.VMEM((16, 2, 2, 2, 8, 16, 128), bf16),
            pltpu.VMEM((2, 2, 2, 8, 16, 16, 128), bf16),
            pltpu.VMEM((2, 256, 512), bf16),
            pltpu.VMEM((128, 256), bf16),
            pltpu.VMEM((16, 512), jnp.int32),
            pltpu.VMEM((2, 4, 2, 256, 128), bf16),
            pltpu.VMEM((4, 64, 256), f32),
            pltpu.VMEM((8, 256, 256), bf16),
            pltpu.VMEM((2, 8, 256, 256), bf16),
            pltpu.VMEM((CHUNKS, 2, 2, 2, 64, 256), f32),
            pltpu.VMEM((CHUNKS, 2, 2, 2, 64, 256), bf16),
            pltpu.VMEM((CHUNKS, 2, 2, 2, 64, 256), bf16),
            pltpu.VMEM((CHUNKS, 2, 3, 64, 256), f32),
            pltpu.VMEM((CHUNKS, 2, 3, 64, 256), bf16),
            pltpu.VMEM((CHUNKS, 2, 3, 64, 256), bf16),
            pltpu.VMEM((CHUNKS, 2, 2, 64, 256), bf16),
            pltpu.VMEM((CHUNKS, 2, 2, 64, 256), bf16),
            pltpu.VMEM((CHUNKS, 2, 2, 64, 256), bf16),
            pltpu.VMEM((CHUNKS, 2, 64, 256), bf16),
            pltpu.VMEM((4, 8, 64, 256), bf16),
            pltpu.VMEM((4, 8, 64, 256), bf16),
            pltpu.VMEM((2, 8, 64, 256), bf16),
            pltpu.VMEM((4, 128, 16, 128), f32),
            pltpu.SemaphoreType.DMA((4,)),
            pltpu.SemaphoreType.DMA((3,)),
            pltpu.SemaphoreType.DMA((CHUNKS,)),
            pltpu.SemaphoreType.DMA((CHUNKS,)),
            pltpu.SemaphoreType.DMA((CHUNKS,)),
            pltpu.SemaphoreType.DMA((CHUNKS,)),
            pltpu.SemaphoreType.DMA((CHUNKS, 8)),
            pltpu.SemaphoreType.DMA((CHUNKS, 8)),
        ]
        + [pltpu.SemaphoreType.DMA((CHUNKS, 2))] * 12
        + [pltpu.SemaphoreType.DMA],
        compiler_params=pltpu.CompilerParams(
            collective_id=0, has_side_effects=True, vmem_limit_bytes=50 << 20
        ),
    )(
        echoes.reshape(256, 4, 16, 128),
        *[pltpu.with_memory_space_constraint(array, pltpu.HBM) for array in small],
    )


def solution(mesh):
    placed = (P(None, "wide", None, "grp"), P(), P())
    return jax.shard_map(
        shards, mesh=mesh, in_specs=placed, out_specs=P("grp", None, "wide", None), check_vma=False
    )
```

```python
import math

import jax
import jax.numpy as jnp
import ml_dtypes
import numpy as np
from jax import lax
from jax.experimental import pallas as pl
from jax.experimental.pallas import tpu as pltpu
from jax.sharding import PartitionSpec as P

MESH = pl.DeviceIdType.MESH
CHUNKS = 4


def doppler_operator(length, wide):
    index = np.arange(length, dtype=np.int32)
    phases = index[:, None] * index[None, :] % length
    angles = phases.astype(np.float32) * np.float32(2.0 * math.pi / length)
    scale = np.float32(1.0 / math.sqrt(length))
    cosine = np.cos(angles) * scale
    sine = -np.sin(angles) * scale
    table = np.array([[cosine, -sine], [sine, cosine]], np.float32)
    table = table.transpose(0, 2, 1, 3).reshape(2, length, 2, wide, length // wide)
    full = np.zeros((2, 2, length, wide, 2, 2, length // wide), np.float32)
    for gate in range(2):
        full[:, gate, :, :, gate] = table.transpose(0, 1, 3, 2, 4)
    return full.reshape(4 * length, 4 * length).T.reshape(2, 2 * length, 4 * length).astype(ml_dtypes.bfloat16)


def kernel(
    echoes, patterns, choice, operator, out,
    raw, single, turned, mid, held, oper, pats, picks, weights, mine, give, got, keep, pass_on, passed, keep_odd,
    pass_odd, passed_odd, to_mid, sums, near, far, home, home_odd, home_mid, spread, odd_bins,
    load_sem, in_sem, z_send, z_recv, xy_send, xy_recv, swap_send, swap_recv, pass_send, pass_recv, odd_send, odd_recv,
    mid_send, mid_recv, sums_send, sums_recv, near_send, near_recv, far_send, far_recv, out_sem,
):
    grp, wide = lax.axis_index("grp"), lax.axis_index("wide")
    high, core = grp // 2, grp % 2
    low, place = wide // 16, wide % 16
    row, column = place // 4, place % 4
    plane = high * 2 + low

    def at(to_plane, to_place, to_core):
        return {"grp": (to_plane // 2) * 2 + to_core, "wide": (to_plane % 2) * 16 + to_place}

    def away(step):
        return (plane + step + 8) % 8

    def around(step):
        return ((row + step // 4) % 4) * 4 + (column + step % 4) % 4

    def await_all(ref, sem):
        pltpu.make_async_copy(ref, ref, sem).wait()

    quarters = [(high + step) % 4 for step in (1, 2, 3, 0)]
    loads = [
        pltpu.make_async_copy(echoes.at[:, quarter], raw.at[n], load_sem.at[n])
        for n, quarter in enumerate(quarters)
    ]
    small = [
        pltpu.make_async_copy(a, b, in_sem.at[n])
        for n, (a, b) in enumerate([(choice, picks), (patterns, pats), (operator, oper)])
    ]
    loads[0].start()

    barrier = pltpu.get_barrier_semaphore()

    def greet(device):
        pl.semaphore_signal(barrier, inc=1, device_id=device, device_id_type=MESH)

    for step in (-3, -2, -1, 1, 2, 3):
        greet(at(away(step), place, core))
    for step in range(1, 16):
        greet(at(plane, around(step), core))
    greet(at(plane, place, 1 - core))

    for load in loads[1:] + small:
        load.start()

    def turn(n, block):
        slot = block % 4
        for ip in range(8):
            single[slot, ip] = raw[n, ip * 32 + block].astype(jnp.float32)
        for pair in range(8):
            both = jnp.concatenate([single[slot, :, pair * 2], single[slot, :, pair * 2 + 1]], axis=0)
            turned[block % 16, block // 16, quarters[n], pair] = both.astype(jnp.bfloat16)

    def of(chunk):
        return pl.ds(chunk * 2, 2)

    def send_z(chunk, side):
        pltpu.make_async_remote_copy(
            src_ref=turned.at[:, :, quarters[side], of(chunk)],
            dst_ref=mid.at[:, side, 1, :, of(chunk)],
            send_sem=z_send.at[chunk],
            recv_sem=z_recv.at[chunk],
            device_id=at(away(2 - 4 * side), place, core),
            device_id_type=MESH,
        ).start()

    for n in range(4):
        loads[n].wait()

        def turn_some(some, carry):
            for block in range(4):
                turn(n, some * 4 + block)
            return carry

        lax.fori_loop(0, 8, turn_some, 0)
        if n == 0:
            pl.semaphore_wait(barrier, 22)
        for chunk in range(CHUNKS):
            if n < 2:
                if chunk < 2:
                    send_z(chunk, n)
            else:
                side = 3 - n
                pltpu.make_async_copy(
                    turned.at[:, :, quarters[n], of(chunk)], mid.at[:, side, 0, :, of(chunk)], z_recv.at[chunk]
                ).start()

    def send_xy(chunk):
        await_all(mid.at[:, :, :, :, of(chunk)], z_recv.at[chunk])

        @pl.when(chunk < CHUNKS - 2)
        def _():
            for side in range(2):
                send_z(chunk + 2, side)

        def one(step, carry):
            to = around(step)
            pltpu.make_async_remote_copy(
                src_ref=mid.at[to, :, :, :, of(chunk)],
                dst_ref=held.at[:, :, :, of(chunk), place],
                send_sem=xy_send.at[chunk],
                recv_sem=xy_recv.at[chunk],
                device_id=at(plane, to, core),
                device_id_type=MESH,
            ).start()
            return carry

        lax.fori_loop(1, 16, one, 0)
        pltpu.make_async_copy(
            mid.at[place, :, :, :, of(chunk)], held.at[:, :, :, of(chunk), place], xy_recv.at[chunk]
        ).start()

    for load in small:
        load.wait()
    lane = lax.broadcasted_iota(jnp.int32, (512, 128), 1)
    number = lax.broadcasted_iota(jnp.int32, (256, 512), 0)
    for h in range(4):
        found = []
        for j in range(2):
            n = h * 4 + j
            pick = jnp.where(core == 0, picks[n : n + 1, :], picks[n + 2 : n + 3, :])
            hot = (pick == number).astype(jnp.float32).astype(jnp.bfloat16)
            found.append(jnp.dot(pats[...], hot, preferred_element_type=jnp.float32).T)
        real = jnp.where(lane < 64, found[0], pltpu.roll(found[1], 64, 1)).astype(jnp.bfloat16)
        imag = jnp.where(lane < 64, pltpu.roll(found[0], 64, 1), found[1]).astype(jnp.bfloat16)
        for beams in range(8):
            rows = slice(beams * 64, beams * 64 + 64)
            to = slice((beams // 2) * 64, (beams // 2) * 64 + 64)
            weights[beams % 2, h, 0, to] = real[rows]
            weights[beams % 2, h, 1, to] = imag[rows]

    real_lane = lax.broadcasted_iota(jnp.int32, (256, 256), 1) // 4 % 2 == 0

    def beams_of(owner, chunk, n):
        side, half, pair = n // 4, (low + n // 2) % 2, chunk * 2 + n % 2
        used = [weights[owner, h].reshape(512, 128) for h in (high, (high + 2 * side + 3) % 4)]
        samples = [held[side, unit, half, pair].reshape(256, 128) for unit in range(2)]
        both = lax.dot_general(
            jnp.concatenate(used, axis=1),
            jnp.concatenate(samples, axis=1),
            (((1,), (1,)), ((), ())),
            preferred_element_type=jnp.float32,
        )
        by_real, by_imag = both[:256], both[256:]
        return by_real + jnp.where(real_lane, -pltpu.roll(by_imag, 252, 1), pltpu.roll(by_imag, 4, 1))

    def remote(source, target, send, recv, step):
        return pltpu.make_async_remote_copy(
            src_ref=source,
            dst_ref=target,
            send_sem=send,
            recv_sem=recv,
            device_id=at(away(step), place, core),
            device_id_type=MESH,
        )

    def swap(chunk, n):
        return pltpu.make_async_remote_copy(
            src_ref=give.at[n],
            dst_ref=got.at[chunk % 2, n],
            send_sem=swap_send.at[chunk, n],
            recv_sem=swap_recv.at[chunk, n],
            device_id=at(plane, place, 1 - core),
            device_id_type=MESH,
        )

    def partials(chunk):
        await_all(held.at[:, :, :, of(chunk)], xy_recv.at[chunk])

        def first(n, carry):
            give[n] = beams_of(1 - core, chunk, n).astype(jnp.bfloat16)
            swap(chunk, n).start()
            return carry

        def second(side, carry):
            ahead = 2 * side - 1
            for other in range(2):
                for j in range(2):
                    n = side * 4 + other * 2 + j
                    mine[...] = beams_of(core, chunk, n).reshape(4, 64, 256)
                    swap(chunk, n).wait()

                    def combined(step):
                        h = away(step) // 2
                        rows = pl.ds(pl.multiple_of(h * 64, 64), 64)
                        return mine[h] + got[chunk % 2, n, rows].astype(jnp.float32)

                    if other == 0:
                        for e in range(2):
                            keep[chunk, side, j, e] = combined(ahead * 2 * e)
                            pass_on[chunk, side, j, e] = combined(-ahead * (2 + 2 * e)).astype(jnp.bfloat16)
                    else:
                        keep_odd[chunk, side, j] = combined(ahead)
                        pass_odd[chunk, side, j] = combined(-ahead * 3).astype(jnp.bfloat16)
                        to_mid[chunk, side, j] = combined(-ahead).astype(jnp.bfloat16)

                        @pl.when(side == j)
                        def _():
                            keep_odd[chunk, side, 2] = combined(ahead * 3)

                        @pl.when(side != j)
                        def _():
                            pass_odd[chunk, side, 2] = combined(ahead * 3).astype(jnp.bfloat16)

            remote(
                pass_on.at[chunk, side], passed.at[chunk, 1 - side],
                pass_send.at[chunk, side], pass_recv.at[chunk, 1 - side], -2 * ahead,
            ).start()
            remote(
                pass_odd.at[chunk, side], passed_odd.at[chunk, 1 - side],
                odd_send.at[chunk, side], odd_recv.at[chunk, 1 - side], -2 * ahead,
            ).start()
            remote(
                to_mid.at[chunk, side], home_mid.at[side, of(chunk)],
                mid_send.at[chunk, side], mid_recv.at[chunk, side], -ahead,
            ).start()
            return carry

        lax.fori_loop(0, 8, first, 0)
        lax.fori_loop(0, 2, second, 0)

    def combine(chunk):
        for side in range(2):
            ahead = 2 * side - 1
            await_all(passed_odd.at[chunk, side], odd_recv.at[chunk, side])
            both = keep_odd[chunk, side] + passed_odd[chunk, side].astype(jnp.float32)
            far[chunk, side] = both[2].astype(jnp.bfloat16)
            remote(
                far.at[chunk, side], home_odd.at[1, chunk * 2 + side],
                far_send.at[chunk, side], far_recv.at[chunk, side], 3 * ahead,
            ).start()
            near[chunk, side] = both[:2].astype(jnp.bfloat16)
            remote(
                near.at[chunk, side], home_odd.at[2 * side, of(chunk)],
                near_send.at[chunk, side], near_recv.at[chunk, side], ahead,
            ).start()
            await_all(passed.at[chunk, side], pass_recv.at[chunk, side])
            for j in range(2):
                both = keep[chunk, side, j] + passed[chunk, side, j].astype(jnp.float32)
                home[3 * side, chunk * 2 + j] = both[0].astype(jnp.bfloat16)
                sums[chunk, side, j] = both[1].astype(jnp.bfloat16)
            remote(
                sums.at[chunk, side], home.at[1 + side, of(chunk)],
                sums_send.at[chunk, side], sums_recv.at[chunk, side], 2 * ahead,
            ).start()

    send_xy(0)

    def forward(chunk, carry):
        @pl.when(chunk < CHUNKS - 1)
        def _():
            send_xy(chunk + 1)

        for late in range(2, CHUNKS):

            @pl.when(chunk == late)
            def _():
                combine(late - 2)

        partials(chunk)
        return carry

    lax.fori_loop(0, CHUNKS, forward, 0)
    combine(CHUNKS - 2)
    combine(CHUNKS - 1)

    for chunk in range(CHUNKS):
        for side in range(2):
            await_all(home_mid.at[side, of(chunk)], mid_recv.at[chunk, side])
            await_all(home_odd.at[2 * side, of(chunk)], near_recv.at[chunk, side])
            await_all(home_odd.at[1, chunk * 2 + side], far_recv.at[chunk, side])
        both = home_mid[0, of(chunk)].astype(jnp.float32) + home_mid[1, of(chunk)].astype(jnp.float32)
        home_odd[3, of(chunk)] = both.astype(jnp.bfloat16)
        for slot in (1, 2):
            others = home_odd[(slot + 4 - low) % 4, of(chunk)].reshape(128, 256)
            odd_bins[slot - 1] = jnp.dot(others, oper[1 - low], preferred_element_type=jnp.float32)
        for slot in (0, 3, 1, 2):
            quarter = (high + slot) % 4
            if slot in (1, 2):
                await_all(home.at[slot, of(chunk)], sums_recv.at[chunk, slot - 1])
            same = home[slot, of(chunk)].reshape(128, 256)
            bins = jnp.dot(same, oper[low], preferred_element_type=jnp.float32)
            if slot in (1, 2):
                bins += odd_bins[slot - 1]
            else:
                others = home_odd[(slot + 4 - low) % 4, of(chunk)].reshape(128, 256)
                bins += jnp.dot(others, oper[1 - low], preferred_element_type=jnp.float32)
            for j in range(2):
                for o in range(2):
                    for gate in range(2):
                        piece = bins[j * 64 : j * 64 + 64, (o * 2 + gate) * 128 : (o * 2 + gate) * 128 + 128]
                        spread[quarter, o * 64 : o * 64 + 64, (chunk * 2 + j) * 2 + gate, :] = piece
            if chunk == CHUNKS - 1:
                raw[quarter, :128] = spread[quarter].astype(jnp.bfloat16)
                for o in range(2):
                    pltpu.make_async_copy(
                        raw.at[quarter, pl.ds(o * 64, 64)],
                        out.at[:, o, pl.ds(pl.multiple_of(quarter * 16, 16), 16)],
                        out_sem,
                    ).start()

    for chunk in range(CHUNKS):
        await_all(turned.at[:, :, pl.ds(0, 2), of(chunk)], z_send.at[chunk])
        await_all(mid.at[pl.ds(0, 15), :, :, :, of(chunk)], xy_send.at[chunk])
        for side in range(2):
            for ref, sem in (
                (pass_on, pass_send), (pass_odd, odd_send), (to_mid, mid_send), (sums, sums_send), (near, near_send),
                (far, far_send),
            ):
                await_all(ref.at[chunk, side], sem.at[chunk, side])
    await_all(out, out_sem)


def shards(echoes, patterns, block_choice):
    bf16, f32 = jnp.bfloat16, jnp.float32
    anywhere = pl.BlockSpec(memory_space=pl.ANY)
    small = [
        patterns.transpose(1, 2, 0).reshape(128, 256),
        block_choice.T,
        jnp.asarray(doppler_operator(128, 32)),
    ]
    return pl.pallas_call(
        kernel,
        out_shape=jax.ShapeDtypeStruct((64, 2, 64, 128), bf16),
        in_specs=[anywhere] * 4,
        out_specs=anywhere,
        scratch_shapes=[
            pltpu.VMEM((4, 256, 16, 128), bf16),
            pltpu.VMEM((4, 8, 16, 128), f32),
            pltpu.VMEM((16, 2, 4, 8, 16, 128), bf16),
            pltpu.VMEM((16, 2, 2, 2, 8, 16, 128), bf16),
            pltpu.VMEM((2, 2, 2, 8, 16, 16, 128), bf16),
            pltpu.VMEM((2, 256, 512), bf16),
            pltpu.VMEM((128, 256), bf16),
            pltpu.VMEM((16, 512), jnp.int32),
            pltpu.VMEM((2, 4, 2, 256, 128), bf16),
            pltpu.VMEM((4, 64, 256), f32),
            pltpu.VMEM((8, 256, 256), bf16),
            pltpu.VMEM((2, 8, 256, 256), bf16),
            pltpu.VMEM((CHUNKS, 2, 2, 2, 64, 256), f32),
            pltpu.VMEM((CHUNKS, 2, 2, 2, 64, 256), bf16),
            pltpu.VMEM((CHUNKS, 2, 2, 2, 64, 256), bf16),
            pltpu.VMEM((CHUNKS, 2, 3, 64, 256), f32),
            pltpu.VMEM((CHUNKS, 2, 3, 64, 256), bf16),
            pltpu.VMEM((CHUNKS, 2, 3, 64, 256), bf16),
            pltpu.VMEM((CHUNKS, 2, 2, 64, 256), bf16),
            pltpu.VMEM((CHUNKS, 2, 2, 64, 256), bf16),
            pltpu.VMEM((CHUNKS, 2, 2, 64, 256), bf16),
            pltpu.VMEM((CHUNKS, 2, 64, 256), bf16),
            pltpu.VMEM((4, 8, 64, 256), bf16),
            pltpu.VMEM((4, 8, 64, 256), bf16),
            pltpu.VMEM((2, 8, 64, 256), bf16),
            pltpu.VMEM((4, 128, 16, 128), f32),
            pltpu.VMEM((2, 128, 512), f32),
            pltpu.SemaphoreType.DMA((4,)),
            pltpu.SemaphoreType.DMA((3,)),
            pltpu.SemaphoreType.DMA((CHUNKS,)),
            pltpu.SemaphoreType.DMA((CHUNKS,)),
            pltpu.SemaphoreType.DMA((CHUNKS,)),
            pltpu.SemaphoreType.DMA((CHUNKS,)),
            pltpu.SemaphoreType.DMA((CHUNKS, 8)),
            pltpu.SemaphoreType.DMA((CHUNKS, 8)),
        ]
        + [pltpu.SemaphoreType.DMA((CHUNKS, 2))] * 12
        + [pltpu.SemaphoreType.DMA],
        compiler_params=pltpu.CompilerParams(
            collective_id=0, has_side_effects=True, vmem_limit_bytes=50 << 20
        ),
    )(
        echoes.reshape(256, 4, 16, 128),
        *[pltpu.with_memory_space_constraint(array, pltpu.HBM) for array in small],
    )


def solution(mesh):
    placed = (P(None, "wide", None, "grp"), P(), P())
    return jax.shard_map(
        shards, mesh=mesh, in_specs=placed, out_specs=P("grp", None, "wide", None), check_vma=False
    )
```

```python
import math

import jax
import jax.numpy as jnp
import ml_dtypes
import numpy as np
from jax import lax
from jax.experimental import pallas as pl
from jax.experimental.pallas import tpu as pltpu
from jax.sharding import PartitionSpec as P

MESH = pl.DeviceIdType.MESH
CHUNKS = 4


def doppler_operator(length, wide):
    index = np.arange(length, dtype=np.int32)
    phases = index[:, None] * index[None, :] % length
    angles = phases.astype(np.float32) * np.float32(2.0 * math.pi / length)
    scale = np.float32(1.0 / math.sqrt(length))
    cosine = np.cos(angles) * scale
    sine = -np.sin(angles) * scale
    table = np.array([[cosine, -sine], [sine, cosine]], np.float32)
    table = table.transpose(0, 2, 1, 3).reshape(2, length, 2, wide, length // wide)
    full = np.zeros((2, 2, length, wide, 2, 2, length // wide), np.float32)
    for gate in range(2):
        full[:, gate, :, :, gate] = table.transpose(0, 1, 3, 2, 4)
    return full.reshape(4 * length, 4 * length).T.reshape(2, 2 * length, 4 * length).astype(ml_dtypes.bfloat16)


def kernel(
    echoes, patterns, choice, operator, out,
    raw, single, turned, mid, held, oper, pats, picks, weights, mine, give, got, keep, pass_on, passed, keep_odd,
    pass_odd, passed_odd, to_mid, sums, near, far, home, home_odd, home_mid, spread, odd_bins,
    load_sem, in_sem, z_send, z_recv, xy_send, xy_recv, swap_send, swap_recv, pass_send, pass_recv, odd_send, odd_recv,
    mid_send, mid_recv, sums_send, sums_recv, near_send, near_recv, far_send, far_recv, out_sem,
):
    grp, wide = lax.axis_index("grp"), lax.axis_index("wide")
    high, core = grp // 2, grp % 2
    low, place = wide // 16, wide % 16
    row, column = place // 4, place % 4
    plane = high * 2 + low

    def at(to_plane, to_place, to_core):
        return {"grp": (to_plane // 2) * 2 + to_core, "wide": (to_plane % 2) * 16 + to_place}

    def away(step):
        return (plane + step + 8) % 8

    def around(step):
        step = step * 7 % 16
        return ((row + step // 4) % 4) * 4 + (column + step % 4) % 4

    def await_all(ref, sem):
        pltpu.make_async_copy(ref, ref, sem).wait()

    quarters = [(high + step) % 4 for step in (1, 2, 3, 0)]
    loads = [
        pltpu.make_async_copy(echoes.at[:, quarter], raw.at[n], load_sem.at[n])
        for n, quarter in enumerate(quarters)
    ]
    small = [
        pltpu.make_async_copy(a, b, in_sem.at[n])
        for n, (a, b) in enumerate([(choice, picks), (patterns, pats), (operator, oper)])
    ]
    loads[0].start()

    barrier = pltpu.get_barrier_semaphore()

    def greet(device):
        pl.semaphore_signal(barrier, inc=1, device_id=device, device_id_type=MESH)

    for step in (-3, -2, -1, 1, 2, 3):
        greet(at(away(step), place, core))
    for step in range(1, 16):
        greet(at(plane, around(step), core))
    greet(at(plane, place, 1 - core))

    for load in loads[1:] + small:
        load.start()

    def turn(n, block):
        slot = block % 4
        for ip in range(8):
            single[slot, ip] = raw[n, ip * 32 + block].astype(jnp.float32)
        for pair in range(8):
            both = jnp.concatenate([single[slot, :, pair * 2], single[slot, :, pair * 2 + 1]], axis=0)
            turned[block % 16, block // 16, quarters[n], pair] = both.astype(jnp.bfloat16)

    def of(chunk):
        return pl.ds(chunk * 2, 2)

    def send_z(chunk, side):
        pltpu.make_async_remote_copy(
            src_ref=turned.at[:, :, quarters[side], of(chunk)],
            dst_ref=mid.at[:, side, 1, :, of(chunk)],
            send_sem=z_send.at[chunk],
            recv_sem=z_recv.at[chunk],
            device_id=at(away(2 - 4 * side), place, core),
            device_id_type=MESH,
        ).start()

    for n in range(4):
        loads[n].wait()

        def turn_some(some, carry):
            for block in range(4):
                turn(n, some * 4 + block)
            return carry

        lax.fori_loop(0, 8, turn_some, 0)
        if n == 0:
            pl.semaphore_wait(barrier, 22)
        for chunk in range(CHUNKS):
            if n < 2:
                if chunk < 2:
                    send_z(chunk, n)
            else:
                side = 3 - n
                pltpu.make_async_copy(
                    turned.at[:, :, quarters[n], of(chunk)], mid.at[:, side, 0, :, of(chunk)], z_recv.at[chunk]
                ).start()

    def send_xy(chunk):
        await_all(mid.at[:, :, :, :, of(chunk)], z_recv.at[chunk])

        @pl.when(chunk < CHUNKS - 2)
        def _():
            for side in range(2):
                send_z(chunk + 2, side)

        def one(step, carry):
            to = around(step)
            pltpu.make_async_remote_copy(
                src_ref=mid.at[to, :, :, :, of(chunk)],
                dst_ref=held.at[:, :, :, of(chunk), place],
                send_sem=xy_send.at[chunk],
                recv_sem=xy_recv.at[chunk],
                device_id=at(plane, to, core),
                device_id_type=MESH,
            ).start()
            return carry

        lax.fori_loop(1, 16, one, 0)
        pltpu.make_async_copy(
            mid.at[place, :, :, :, of(chunk)], held.at[:, :, :, of(chunk), place], xy_recv.at[chunk]
        ).start()

    for load in small:
        load.wait()
    lane = lax.broadcasted_iota(jnp.int32, (512, 128), 1)
    number = lax.broadcasted_iota(jnp.int32, (256, 512), 0)
    for h in range(4):
        found = []
        for j in range(2):
            n = h * 4 + j
            pick = jnp.where(core == 0, picks[n : n + 1, :], picks[n + 2 : n + 3, :])
            hot = (pick == number).astype(jnp.float32).astype(jnp.bfloat16)
            found.append(jnp.dot(pats[...], hot, preferred_element_type=jnp.float32).T)
        real = jnp.where(lane < 64, found[0], pltpu.roll(found[1], 64, 1)).astype(jnp.bfloat16)
        imag = jnp.where(lane < 64, pltpu.roll(found[0], 64, 1), found[1]).astype(jnp.bfloat16)
        for beams in range(8):
            rows = slice(beams * 64, beams * 64 + 64)
            to = slice((beams // 2) * 64, (beams // 2) * 64 + 64)
            weights[beams % 2, h, 0, to] = real[rows]
            weights[beams % 2, h, 1, to] = imag[rows]

    real_lane = lax.broadcasted_iota(jnp.int32, (256, 256), 1) // 4 % 2 == 0

    def beams_of(owner, chunk, n):
        side, half, pair = n // 4, (low + n // 2) % 2, chunk * 2 + n % 2
        used = [weights[owner, h].reshape(512, 128) for h in (high, (high + 2 * side + 3) % 4)]
        samples = [held[side, unit, half, pair].reshape(256, 128) for unit in range(2)]
        both = lax.dot_general(
            jnp.concatenate(used, axis=1),
            jnp.concatenate(samples, axis=1),
            (((1,), (1,)), ((), ())),
            preferred_element_type=jnp.float32,
        )
        by_real, by_imag = both[:256], both[256:]
        return by_real + jnp.where(real_lane, -pltpu.roll(by_imag, 252, 1), pltpu.roll(by_imag, 4, 1))

    def remote(source, target, send, recv, step):
        return pltpu.make_async_remote_copy(
            src_ref=source,
            dst_ref=target,
            send_sem=send,
            recv_sem=recv,
            device_id=at(away(step), place, core),
            device_id_type=MESH,
        )

    def swap(chunk, n):
        return pltpu.make_async_remote_copy(
            src_ref=give.at[n],
            dst_ref=got.at[chunk % 2, n],
            send_sem=swap_send.at[chunk, n],
            recv_sem=swap_recv.at[chunk, n],
            device_id=at(plane, place, 1 - core),
            device_id_type=MESH,
        )

    def partials(chunk):
        await_all(held.at[:, :, :, of(chunk)], xy_recv.at[chunk])

        def first(n, carry):
            give[n] = beams_of(1 - core, chunk, n).astype(jnp.bfloat16)
            swap(chunk, n).start()
            return carry

        def second(side, carry):
            ahead = 2 * side - 1
            for other in range(2):
                for j in range(2):
                    n = side * 4 + other * 2 + j
                    mine[...] = beams_of(core, chunk, n).reshape(4, 64, 256)
                    swap(chunk, n).wait()

                    def combined(step):
                        h = away(step) // 2
                        rows = pl.ds(pl.multiple_of(h * 64, 64), 64)
                        return mine[h] + got[chunk % 2, n, rows].astype(jnp.float32)

                    if other == 0:
                        for e in range(2):
                            keep[chunk, side, j, e] = combined(ahead * 2 * e)
                            pass_on[chunk, side, j, e] = combined(-ahead * (2 + 2 * e)).astype(jnp.bfloat16)
                    else:
                        keep_odd[chunk, side, j] = combined(ahead)
                        pass_odd[chunk, side, j] = combined(-ahead * 3).astype(jnp.bfloat16)
                        to_mid[chunk, side, j] = combined(-ahead).astype(jnp.bfloat16)

                        @pl.when(side == j)
                        def _():
                            keep_odd[chunk, side, 2] = combined(ahead * 3)

                        @pl.when(side != j)
                        def _():
                            pass_odd[chunk, side, 2] = combined(ahead * 3).astype(jnp.bfloat16)

            remote(
                pass_on.at[chunk, side], passed.at[chunk, 1 - side],
                pass_send.at[chunk, side], pass_recv.at[chunk, 1 - side], -2 * ahead,
            ).start()
            remote(
                pass_odd.at[chunk, side], passed_odd.at[chunk, 1 - side],
                odd_send.at[chunk, side], odd_recv.at[chunk, 1 - side], -2 * ahead,
            ).start()
            remote(
                to_mid.at[chunk, side], home_mid.at[side, of(chunk)],
                mid_send.at[chunk, side], mid_recv.at[chunk, side], -ahead,
            ).start()
            return carry

        lax.fori_loop(0, 8, first, 0)
        lax.fori_loop(0, 2, second, 0)

    def combine(chunk):
        for side in range(2):
            ahead = 2 * side - 1
            await_all(passed_odd.at[chunk, side], odd_recv.at[chunk, side])
            both = keep_odd[chunk, side] + passed_odd[chunk, side].astype(jnp.float32)
            far[chunk, side] = both[2].astype(jnp.bfloat16)
            remote(
                far.at[chunk, side], home_odd.at[1, chunk * 2 + side],
                far_send.at[chunk, side], far_recv.at[chunk, side], 3 * ahead,
            ).start()
            near[chunk, side] = both[:2].astype(jnp.bfloat16)
            remote(
                near.at[chunk, side], home_odd.at[2 * side, of(chunk)],
                near_send.at[chunk, side], near_recv.at[chunk, side], ahead,
            ).start()
            await_all(passed.at[chunk, side], pass_recv.at[chunk, side])
            for j in range(2):
                both = keep[chunk, side, j] + passed[chunk, side, j].astype(jnp.float32)
                home[3 * side, chunk * 2 + j] = both[0].astype(jnp.bfloat16)
                sums[chunk, side, j] = both[1].astype(jnp.bfloat16)
            remote(
                sums.at[chunk, side], home.at[1 + side, of(chunk)],
                sums_send.at[chunk, side], sums_recv.at[chunk, side], 2 * ahead,
            ).start()

    send_xy(0)

    def forward(chunk, carry):
        @pl.when(chunk < CHUNKS - 1)
        def _():
            send_xy(chunk + 1)

        for late in range(2, CHUNKS):

            @pl.when(chunk == late)
            def _():
                combine(late - 2)

        partials(chunk)
        return carry

    lax.fori_loop(0, CHUNKS, forward, 0)
    combine(CHUNKS - 2)
    combine(CHUNKS - 1)

    for chunk in range(CHUNKS):
        for side in range(2):
            await_all(home_mid.at[side, of(chunk)], mid_recv.at[chunk, side])
            await_all(home_odd.at[2 * side, of(chunk)], near_recv.at[chunk, side])
            await_all(home_odd.at[1, chunk * 2 + side], far_recv.at[chunk, side])
        both = home_mid[0, of(chunk)].astype(jnp.float32) + home_mid[1, of(chunk)].astype(jnp.float32)
        home_odd[3, of(chunk)] = both.astype(jnp.bfloat16)
        for slot in (1, 2):
            others = home_odd[(slot + 4 - low) % 4, of(chunk)].reshape(128, 256)
            odd_bins[slot - 1] = jnp.dot(others, oper[1 - low], preferred_element_type=jnp.float32)
        for slot in (0, 3, 1, 2):
            quarter = (high + slot) % 4
            if slot in (1, 2):
                await_all(home.at[slot, of(chunk)], sums_recv.at[chunk, slot - 1])
            same = home[slot, of(chunk)].reshape(128, 256)
            bins = jnp.dot(same, oper[low], preferred_element_type=jnp.float32)
            if slot in (1, 2):
                bins += odd_bins[slot - 1]
            else:
                others = home_odd[(slot + 4 - low) % 4, of(chunk)].reshape(128, 256)
                bins += jnp.dot(others, oper[1 - low], preferred_element_type=jnp.float32)
            for j in range(2):
                for o in range(2):
                    for gate in range(2):
                        piece = bins[j * 64 : j * 64 + 64, (o * 2 + gate) * 128 : (o * 2 + gate) * 128 + 128]
                        spread[quarter, o * 64 : o * 64 + 64, (chunk * 2 + j) * 2 + gate, :] = piece
            if chunk == CHUNKS - 1:
                raw[quarter, :128] = spread[quarter].astype(jnp.bfloat16)
                for o in range(2):
                    pltpu.make_async_copy(
                        raw.at[quarter, pl.ds(o * 64, 64)],
                        out.at[:, o, pl.ds(pl.multiple_of(quarter * 16, 16), 16)],
                        out_sem,
                    ).start()

    for chunk in range(CHUNKS):
        await_all(turned.at[:, :, pl.ds(0, 2), of(chunk)], z_send.at[chunk])
        await_all(mid.at[pl.ds(0, 15), :, :, :, of(chunk)], xy_send.at[chunk])
        for side in range(2):
            for ref, sem in (
                (pass_on, pass_send), (pass_odd, odd_send), (to_mid, mid_send), (sums, sums_send), (near, near_send),
                (far, far_send),
            ):
                await_all(ref.at[chunk, side], sem.at[chunk, side])
    await_all(out, out_sem)


def shards(echoes, patterns, block_choice):
    bf16, f32 = jnp.bfloat16, jnp.float32
    anywhere = pl.BlockSpec(memory_space=pl.ANY)
    small = [
        patterns.transpose(1, 2, 0).reshape(128, 256),
        block_choice.T,
        jnp.asarray(doppler_operator(128, 32)),
    ]
    return pl.pallas_call(
        kernel,
        out_shape=jax.ShapeDtypeStruct((64, 2, 64, 128), bf16),
        in_specs=[anywhere] * 4,
        out_specs=anywhere,
        scratch_shapes=[
            pltpu.VMEM((4, 256, 16, 128), bf16),
            pltpu.VMEM((4, 8, 16, 128), f32),
            pltpu.VMEM((16, 2, 4, 8, 16, 128), bf16),
            pltpu.VMEM((16, 2, 2, 2, 8, 16, 128), bf16),
            pltpu.VMEM((2, 2, 2, 8, 16, 16, 128), bf16),
            pltpu.VMEM((2, 256, 512), bf16),
            pltpu.VMEM((128, 256), bf16),
            pltpu.VMEM((16, 512), jnp.int32),
            pltpu.VMEM((2, 4, 2, 256, 128), bf16),
            pltpu.VMEM((4, 64, 256), f32),
            pltpu.VMEM((8, 256, 256), bf16),
            pltpu.VMEM((2, 8, 256, 256), bf16),
            pltpu.VMEM((CHUNKS, 2, 2, 2, 64, 256), f32),
            pltpu.VMEM((CHUNKS, 2, 2, 2, 64, 256), bf16),
            pltpu.VMEM((CHUNKS, 2, 2, 2, 64, 256), bf16),
            pltpu.VMEM((CHUNKS, 2, 3, 64, 256), f32),
            pltpu.VMEM((CHUNKS, 2, 3, 64, 256), bf16),
            pltpu.VMEM((CHUNKS, 2, 3, 64, 256), bf16),
            pltpu.VMEM((CHUNKS, 2, 2, 64, 256), bf16),
            pltpu.VMEM((CHUNKS, 2, 2, 64, 256), bf16),
            pltpu.VMEM((CHUNKS, 2, 2, 64, 256), bf16),
            pltpu.VMEM((CHUNKS, 2, 64, 256), bf16),
            pltpu.VMEM((4, 8, 64, 256), bf16),
            pltpu.VMEM((4, 8, 64, 256), bf16),
            pltpu.VMEM((2, 8, 64, 256), bf16),
            pltpu.VMEM((4, 128, 16, 128), f32),
            pltpu.VMEM((2, 128, 512), f32),
            pltpu.SemaphoreType.DMA((4,)),
            pltpu.SemaphoreType.DMA((3,)),
            pltpu.SemaphoreType.DMA((CHUNKS,)),
            pltpu.SemaphoreType.DMA((CHUNKS,)),
            pltpu.SemaphoreType.DMA((CHUNKS,)),
            pltpu.SemaphoreType.DMA((CHUNKS,)),
            pltpu.SemaphoreType.DMA((CHUNKS, 8)),
            pltpu.SemaphoreType.DMA((CHUNKS, 8)),
        ]
        + [pltpu.SemaphoreType.DMA((CHUNKS, 2))] * 12
        + [pltpu.SemaphoreType.DMA],
        compiler_params=pltpu.CompilerParams(
            collective_id=0, has_side_effects=True, vmem_limit_bytes=50 << 20
        ),
    )(
        echoes.reshape(256, 4, 16, 128),
        *[pltpu.with_memory_space_constraint(array, pltpu.HBM) for array in small],
    )


def solution(mesh):
    placed = (P(None, "wide", None, "grp"), P(), P())
    return jax.shard_map(
        shards, mesh=mesh, in_specs=placed, out_specs=P("grp", None, "wide", None), check_vma=False
    )
```
